256 devices in a mesh: seq: 32 (over y, x, core), tp: 8 (over z).
Axes of the slice: x: 4, y: 4, z: 8, core: 2. Of those that a mesh axis runs over, the one named last changes fastest.
Arguments:
- head_queries: bfloat16 [16384, 8192], P('seq', 'tp'), may hold values from -8 to 8
- key_projection_rows: bfloat16 [16384, 1024], P('seq', 'tp'), may hold values from -8 to 8
- value_projection_rows: bfloat16 [16384, 1024], P('seq', 'tp'), may hold values from -6 to 6
- gate_logit: bfloat16 [16384], P('seq'), may hold values from -8 to 8
- upstream: bfloat16 [16384, 8192], P('seq', 'tp'), may hold values from -16 to 16
- picked: int32 [4096], P('seq'), may hold values from 0 to 512, as said below
Outputs:
- query_grad: bfloat16 [16384, 8192], P('seq', 'tp')
- key_grad: bfloat16 [16384, 1024], P('seq', 'tp')
- value_grad: bfloat16 [16384, 1024], P('seq', 'tp')
- logit_grad: bfloat16 [16384], P('seq')
The draws below stay inside these ranges and needn't reach their ends.
Inputs may be any that keep to these rules, and one draw needn't show every extreme that they name: Block j of 128 entries belongs to seq shard j: that shard's picked local token positions in increasing order, then 512 in every empty slot. 2048 positions are picked in all, and some shard fills all 128 slots.
All inputs are finite; a program needn't handle non-finite values.
Results may differ from the reference program's by a relative error of at most 0.012.
The reference program's roundings to bfloat16 on the way (of `weights_low`, `scaled_low` and `slopes`) count: a program that leaves them out, or rounds other values in their place, can miss the bound.
Values may be sent and summed in bfloat16 or wider, within the bound.
No kernel may reach another device: no remote copies, remote signals or barrier semaphores. Data moves between devices by JAX's collectives and lax.ppermute only.
A program may use at most 128 MiB of HBM per device.

```python
import math
import jax
import jax.numpy as jnp
from jax import lax

QUERY_HEADS = 64
KEY_VALUE_HEADS = 8
HEAD_SIZE = 128
TOK_SHARD = 512
SEQUENCE_LENGTH = 16384
CAP = 128
PICKED_TOKENS = 2048
N_SEQ = 32


def pick_grid_of(key):
    key = jax.random.fold_in(key, 977)
    busy_key, weight_key, rank_key = jax.random.split(key, 3)
    shard_ids = jnp.arange(N_SEQ, dtype=jnp.int32)
    busiest = jax.random.randint(busy_key, (), 0, N_SEQ)
    weights = jnp.where(shard_ids == busiest, 0, jax.random.randint(weight_key, (N_SEQ,), 2, 5))
    remaining = PICKED_TOKENS - CAP
    portion = remaining * weights // jnp.sum(weights)
    others = (shard_ids != busiest).astype(jnp.int32)
    ranking = jnp.cumsum(others) - 1
    leftover = remaining - jnp.sum(portion)
    portion = portion + others * (ranking < leftover).astype(jnp.int32)
    counts = jnp.where(shard_ids == busiest, CAP, portion)
    scores = jax.random.randint(rank_key, (N_SEQ, TOK_SHARD), 0, 65536) * TOK_SHARD + jnp.arange(TOK_SHARD, dtype=jnp.int32)[None, :]
    ordering = jnp.argsort(jnp.argsort(scores, axis=1), axis=1)
    picked_positions = jnp.arange(TOK_SHARD, dtype=jnp.int32)[None, :]
    chosen = ordering < counts[:, None]
    pick_grid = jnp.sort(jnp.where(chosen, picked_positions, TOK_SHARD), axis=1)[:, :CAP]
    return pick_grid.astype(jnp.int32)


def draw_picked(key, part):
    return pick_grid_of(key).reshape(-1)


def draw_head_queries(key, part):
    key = jax.random.fold_in(key, 11)
    return jax.random.truncated_normal(key, -6.0, 6.0, (SEQUENCE_LENGTH, QUERY_HEADS * HEAD_SIZE), jnp.float32).astype(jnp.bfloat16)


def draw_key_projection_rows(key, part):
    key = jax.random.fold_in(key, 12)
    return jax.random.truncated_normal(key, -6.0, 6.0, (SEQUENCE_LENGTH, KEY_VALUE_HEADS * HEAD_SIZE), jnp.float32).astype(jnp.bfloat16)


def draw_upstream(key, part):
    key = jax.random.fold_in(key, 13)
    columns = jnp.arange(QUERY_HEADS * HEAD_SIZE, dtype=jnp.float32) / (QUERY_HEADS * HEAD_SIZE - 1)
    sampled_tensor = jax.random.truncated_normal(key, -6.0, 6.0, (SEQUENCE_LENGTH, QUERY_HEADS * HEAD_SIZE), jnp.float32)
    return (0.25 * sampled_tensor * (3.0 ** columns)[None, :]).astype(jnp.bfloat16)


def block_scale(key, extent, cuts, smallest, top_value):
    def one(position, parts):
        heights = jax.random.uniform(jax.random.fold_in(jax.random.fold_in(key, 6), position), (parts,), jnp.float32, smallest / len(cuts), top_value / len(cuts))
        return jnp.repeat(jnp.exp(heights), extent[position] // parts).reshape((-1,) + (1,) * (len(extent) - position - 1))

    level = one(*cuts[0])
    for cut in cuts[1:]:
        level = level * one(*cut)
    return level


def gaussian(key, shape, spread, bound, pieces=(), kind=jnp.bfloat16):
    factor_of = block_scale(key, shape, pieces, -0.22, 0.18) if pieces else 1.0
    entries = jax.random.normal(key, shape, jnp.float32) * spread * factor_of
    return jnp.minimum(jnp.maximum(entries, -bound), bound).astype(kind)


def setup_inputs(seed: int = 0) -> dict:
    key_list = jax.random.split(jax.random.key(seed), 7)
    return {
        "head_queries": draw_head_queries(jax.random.fold_in(key_list[6], 71), 0),
        "key_projection_rows": draw_key_projection_rows(jax.random.fold_in(key_list[6], 71), 0),
        "value_projection_rows": gaussian(key_list[2], (SEQUENCE_LENGTH, KEY_VALUE_HEADS * HEAD_SIZE), 1.0, 6.0, ((0, 32), (1, 8))),
        "gate_logit": gaussian(key_list[3], (SEQUENCE_LENGTH,), 2.0, 8.0, ((0, 32),)),
        "upstream": draw_upstream(jax.random.fold_in(key_list[6], 71), 0),
        "picked": draw_picked(jax.random.fold_in(key_list[6], 71), 0),
    }


def reference(head_queries, key_projection_rows, value_projection_rows, gate_logit, upstream, picked):
    span_length = head_queries.shape[0]
    pick_grid = picked.reshape(N_SEQ, CAP)
    offsets = (jnp.arange(N_SEQ, dtype=jnp.int32) * TOK_SHARD)[:, None]
    located = jnp.where(pick_grid < TOK_SHARD, pick_grid + offsets, span_length).reshape(-1)
    picked_positions = jnp.sort(located)[:PICKED_TOKENS].astype(jnp.int32)
    switch = jax.nn.sigmoid(gate_logit[picked_positions].astype(jnp.float32))
    queries = head_queries[picked_positions].reshape(PICKED_TOKENS, QUERY_HEADS, HEAD_SIZE)
    picked_key_rows = key_projection_rows[picked_positions].reshape(PICKED_TOKENS, KEY_VALUE_HEADS, HEAD_SIZE)
    picked_value_rows = value_projection_rows[picked_positions].reshape(PICKED_TOKENS, KEY_VALUE_HEADS, HEAD_SIZE)
    incoming = upstream[picked_positions].astype(jnp.float32).reshape(PICKED_TOKENS, QUERY_HEADS, HEAD_SIZE)
    scaled = incoming * switch[:, None, None]
    scaled_low = scaled.astype(jnp.bfloat16)
    causal = picked_positions[None, :] <= picked_positions[:, None]
    factor = 1.0 / math.sqrt(HEAD_SIZE)
    query_group_width = QUERY_HEADS // KEY_VALUE_HEADS

    def one_head(number):
        family = number // query_group_width
        query_part = lax.dynamic_index_in_dim(queries, number, 1, keepdims=False)
        key_part = lax.dynamic_index_in_dim(picked_key_rows, family, 1, keepdims=False)
        value_part = lax.dynamic_index_in_dim(picked_value_rows, family, 1, keepdims=False)
        incoming_part = lax.dynamic_index_in_dim(incoming, number, 1, keepdims=False)
        scaled_part = lax.dynamic_index_in_dim(scaled, number, 1, keepdims=False)
        scaled_low_part = lax.dynamic_index_in_dim(scaled_low, number, 1, keepdims=False)
        scores = jnp.dot(query_part, key_part.T, preferred_element_type=jnp.float32) * factor
        scores = jnp.where(causal, scores, -1e+30)
        highest = lax.optimization_barrier(jnp.max(scores, axis=1, keepdims=True))
        raised = jnp.exp(scores - highest)
        weights = raised / lax.optimization_barrier(jnp.sum(raised, axis=1, keepdims=True))
        weights_low = weights.astype(jnp.bfloat16)
        attended = jnp.dot(weights_low, value_part, preferred_element_type=jnp.float32)
        products = lax.optimization_barrier(jnp.sum(incoming_part * attended, axis=1))
        deltas = lax.optimization_barrier(jnp.sum(scaled_part * attended, axis=1, keepdims=True))
        pushed = jnp.dot(scaled_low_part, value_part.T, preferred_element_type=jnp.float32)
        slopes = (weights * (pushed - deltas)).astype(jnp.bfloat16)
        query_part_grad = jnp.dot(slopes, key_part, preferred_element_type=jnp.float32) * factor
        key_part_grad = jnp.dot(slopes.T, query_part, preferred_element_type=jnp.float32) * factor
        value_part_grad = jnp.dot(weights_low.T, scaled_low_part, preferred_element_type=jnp.float32)
        return (query_part_grad, key_part_grad, value_part_grad, products)
    query_all, gathered_keys, gathered_values, products = lax.map(one_head, jnp.arange(QUERY_HEADS, dtype=jnp.int32))
    key_grad_total = gathered_keys.reshape(KEY_VALUE_HEADS, query_group_width, PICKED_TOKENS, HEAD_SIZE).sum(axis=1)
    value_grad_total = gathered_values.reshape(KEY_VALUE_HEADS, query_group_width, PICKED_TOKENS, HEAD_SIZE).sum(axis=1)
    query_flat = jnp.transpose(query_all, (1, 0, 2)).reshape(PICKED_TOKENS, QUERY_HEADS * HEAD_SIZE).astype(jnp.bfloat16)
    flattened_keys = jnp.transpose(key_grad_total, (1, 0, 2)).reshape(PICKED_TOKENS, KEY_VALUE_HEADS * HEAD_SIZE).astype(jnp.bfloat16)
    flattened_values = jnp.transpose(value_grad_total, (1, 0, 2)).reshape(PICKED_TOKENS, KEY_VALUE_HEADS * HEAD_SIZE).astype(jnp.bfloat16)
    logit_rows = (switch * (1.0 - switch) * lax.optimization_barrier(jnp.sum(products, axis=0))).astype(jnp.bfloat16)
    query_out = jnp.zeros((span_length, QUERY_HEADS * HEAD_SIZE), jnp.bfloat16).at[picked_positions].set(query_flat)
    key_result = jnp.zeros((span_length, KEY_VALUE_HEADS * HEAD_SIZE), jnp.bfloat16).at[picked_positions].set(flattened_keys)
    value_result = jnp.zeros((span_length, KEY_VALUE_HEADS * HEAD_SIZE), jnp.bfloat16).at[picked_positions].set(flattened_values)
    logit_out = jnp.zeros((span_length,), jnp.bfloat16).at[picked_positions].set(logit_rows)
    return (query_out, key_result, value_result, logit_out)
```

```python
import functools
import math

import jax
import jax.numpy as jnp
from jax import lax
from jax.experimental import pallas as pl
from jax.experimental.pallas import tpu as pltpu
from jax.sharding import Mesh, PartitionSpec as P

QUERY_HEADS = 64
KEY_VALUE_HEADS = 8
HEAD = 128
SLOTS = 128
TOKENS = 512
CHIPS = 16
PICKED = 2048
GROUP = QUERY_HEADS // KEY_VALUE_HEADS
FACTOR = 1.0 / math.sqrt(HEAD)
LOG_FACTOR = FACTOR * math.log2(math.e)
CHUNK = 32
CHUNKS = SLOTS // CHUNK
ROWS = GROUP * CHUNK
KEYS = 512
SENTINEL = 128.0
LIVE_BELOW = 32.0
NEGATIVE = -1e30
F32 = jnp.float32
BF16 = jnp.bfloat16
VMEM_BYTES = 48 * 1024 * 1024


def nt_dot(a, b):
    return lax.dot_general(a, b, (((1,), (1,)), ((), ())), preferred_element_type=F32)


def tn_dot(a, b):
    return lax.dot_general(a, b, (((0,), (0,)), ((), ())), preferred_element_type=F32)


def place_matrix(picked):
    token = lax.broadcasted_iota(jnp.int32, (TOKENS, SLOTS), 0)
    return jnp.where(token == picked, 1.0, 0.0).astype(F32)


def switch_of(gate, gather):
    rows = jnp.dot(
        jnp.broadcast_to(gate, (16, TOKENS)), gather.astype(BF16), preferred_element_type=F32
    )
    return 1.0 / (1.0 + jnp.exp(-rows))


def pick_kernel(picked_ref, gate_ref, k_ref, v_ref, q_ref, up_ref, kv_out, qs_out):
    placed = place_matrix(picked_ref[...])
    gather = placed.T.astype(BF16)
    slot_dead = (
        jnp.broadcast_to(
            jnp.where(picked_ref[...] >= TOKENS, 1.0, 0.0).astype(F32), (SLOTS, SLOTS)
        ).T
        * SENTINEL
    )
    switch = jnp.broadcast_to(switch_of(gate_ref[...], placed)[0:1], (SLOTS, SLOTS)).T
    keys = (jnp.dot(gather, k_ref[...], preferred_element_type=F32) + slot_dead).astype(BF16)
    values = jnp.dot(gather, v_ref[...], preferred_element_type=F32).astype(BF16)
    for chip in range(CHIPS):
        kv_out[chip, :, 0:HEAD] = keys
        kv_out[chip, :, HEAD : 2 * HEAD] = values
    for h in range(GROUP):
        lanes = slice(h * HEAD, (h + 1) * HEAD)
        q_rows = jnp.dot(gather, q_ref[:, lanes], preferred_element_type=F32)
        q_rows = (q_rows + slot_dead).astype(BF16)
        up_rows = jnp.dot(gather, up_ref[:, lanes], preferred_element_type=F32)
        scaled = (up_rows * switch).astype(BF16)
        for t in range(CHUNKS):
            rows = slice(t * CHUNK, (t + 1) * CHUNK)
            qs_out[0, t, h * CHUNK : (h + 1) * CHUNK, :] = q_rows[rows]
            qs_out[1, t, h * CHUNK : (h + 1) * CHUNK, :] = scaled[rows]


def count_live(block):
    live = jnp.where(block.astype(F32) < LIVE_BELOW, 1.0, 0.0)
    return jnp.sum(live, axis=0, keepdims=True)[0, 0].astype(jnp.int32)


def row_limit(t, offset, count, core):
    lane = lax.broadcasted_iota(jnp.int32, (1, ROWS), 1)
    own = offset + (t % CHUNKS) * CHUNK + lax.rem(lane, CHUNK) + 1
    other = offset + jnp.where(core == 0, count, 0)
    return jnp.where(t < CHUNKS, own, other)


def stats_kernel(kv_ref, own_ref, oth_ref, kc_out, vc_out, stats_out, info_out, k_pack, v_pack):
    chip = lax.axis_index("y") * 4 + lax.axis_index("x")
    core = lax.axis_index("c")
    k_pack[...] = jnp.zeros_like(k_pack)
    v_pack[...] = jnp.zeros_like(v_pack)
    offset = 0
    own_offset = 0
    own_count = 0
    counts = [count_live(kv_ref[s, :, 0:HEAD]) for s in range(CHIPS)]
    for s in range(CHIPS):
        k_pack[pl.ds(offset, SLOTS), :] = kv_ref[s, :, 0:HEAD].astype(F32)
        v_pack[pl.ds(offset, SLOTS), :] = kv_ref[s, :, HEAD : 2 * HEAD].astype(F32)
        info_out[s] = jnp.asarray(offset, jnp.int32)
        own_offset = jnp.where(chip == s, offset, own_offset)
        own_count = jnp.where(chip == s, counts[s], own_count)
        offset = offset + counts[s]
    other_count = 0
    for t in range(CHUNKS):
        other_count += count_live(oth_ref[0, t, 0:CHUNK, :])
    info_out[16] = own_offset
    info_out[17] = own_count
    info_out[18] = other_count
    kc_out[...] = k_pack[0:PICKED, :].astype(BF16)
    vc_out[...] = v_pack[0:PICKED, :].astype(BF16)
    stats_out[...] = jnp.zeros_like(stats_out)
    blocks = lax.div(own_offset + own_count + KEYS - 1, KEYS)
    key_index = lax.broadcasted_iota(jnp.int32, (KEYS, ROWS), 0)

    def attend(t, ref, live_count):
        tt = lax.rem(t, CHUNKS)

        @pl.when(tt * CHUNK < live_count)
        def _():
            limit = row_limit(t, own_offset, own_count, core)
            q_rows = ref[0, tt]
            s_rows = ref[1, tt]

            def step(b, carry):
                top, total, pull = carry
                base = pl.multiple_of(b * KEYS, KEYS)
                scores = nt_dot(kc_out[pl.ds(base, KEYS), :], q_rows) * LOG_FACTOR
                scores = jnp.where(key_index < limit - base, scores, NEGATIVE)
                pushed = nt_dot(vc_out[pl.ds(base, KEYS), :], s_rows)
                new_top = jnp.maximum(top, jnp.max(scores, axis=0, keepdims=True))
                raised = jnp.exp2(scores - new_top)
                fade = jnp.exp2(top - new_top)
                total = total * fade + jnp.sum(raised, axis=0, keepdims=True)
                pull = pull * fade + jnp.sum(raised * pushed, axis=0, keepdims=True)
                return new_top, total, pull

            zero = jnp.zeros((1, ROWS), F32)
            top, total, pull = lax.fori_loop(
                0, blocks, step, (jnp.full((1, ROWS), NEGATIVE, F32), zero, zero)
            )
            stats_out[t, 0:1, :] = top
            stats_out[t, 1:2, :] = total
            stats_out[t, 2:3, :] = pull

    lax.fori_loop(0, CHUNKS, lambda t, _: (attend(t, own_ref, own_count), 0)[1], 0)
    lax.fori_loop(CHUNKS, 2 * CHUNKS, lambda t, _: (attend(t, oth_ref, other_count), 0)[1], 0)


def grad_kernel(
    info_ref,
    kc_ref,
    vc_ref,
    own_ref,
    oth_ref,
    stats_ref,
    peer_ref,
    dkv_out,
    dq_own,
    dq_oth,
    delta_out,
    dk_sum,
    dv_sum,
    dq_sum,
):
    core = lax.axis_index("c")
    own_offset = info_ref[16]
    own_count = info_ref[17]
    other_count = info_ref[18]
    blocks = lax.div(own_offset + own_count + KEYS - 1, KEYS)
    dk_sum[...] = jnp.zeros_like(dk_sum)
    dv_sum[...] = jnp.zeros_like(dv_sum)
    dq_own[...] = jnp.zeros_like(dq_own)
    dq_oth[...] = jnp.zeros_like(dq_oth)
    delta_out[...] = jnp.zeros_like(delta_out)
    key_index = lax.broadcasted_iota(jnp.int32, (KEYS, ROWS), 0)

    def push_back(t, ref, live_count, is_own):
        tt = lax.rem(t, CHUNKS)

        @pl.when(tt * CHUNK < live_count)
        def _():
            limit = row_limit(t, own_offset, own_count, core)
            q_rows = ref[0, tt]
            s_rows = ref[1, tt]
            mine = stats_ref[t]
            theirs = peer_ref[lax.rem(t + CHUNKS, 2 * CHUNKS)]
            top = jnp.maximum(mine[0:1], theirs[0:1])
            mine_scale = jnp.exp2(mine[0:1] - top)
            their_scale = jnp.exp2(theirs[0:1] - top)
            total = mine[1:2] * mine_scale + theirs[1:2] * their_scale
            delta = (mine[2:3] * mine_scale + theirs[2:3] * their_scale) / total
            level = top + jnp.log2(total)
            if is_own:
                half = delta[:, 0:128] + delta[:, 128:256]
                half = half + pltpu.roll(half, 64, 1)
                half = half + pltpu.roll(half, 32, 1)
                lane = lax.broadcasted_iota(jnp.int32, (1, SLOTS), 1)
                delta_out[0:1, :] += jnp.where(lax.div(lane, CHUNK) == tt, half, 0.0)
            dq_sum[...] = jnp.zeros_like(dq_sum)

            def step(b, _):
                base = pl.multiple_of(b * KEYS, KEYS)
                keys = kc_ref[pl.ds(base, KEYS), :]
                scores = nt_dot(keys, q_rows) * LOG_FACTOR
                weights = jnp.where(
                    key_index < limit - base, jnp.exp2(scores - level), 0.0
                )
                pushed = nt_dot(vc_ref[pl.ds(base, KEYS), :], s_rows)
                slopes = (weights * (pushed - delta)).astype(BF16)
                dv_sum[pl.ds(base, KEYS), :] += jnp.dot(
                    weights.astype(BF16), s_rows, preferred_element_type=F32
                )
                dk_sum[pl.ds(base, KEYS), :] += jnp.dot(
                    slopes, q_rows, preferred_element_type=F32
                )
                dq_sum[...] += tn_dot(slopes, keys)
                return 0

            lax.fori_loop(0, blocks, step, 0)
            if is_own:
                dq_own[tt] = dq_sum[...]
            else:
                dq_oth[tt] = dq_sum[...].astype(BF16)

    lax.fori_loop(0, CHUNKS, lambda t, _: (push_back(t, own_ref, own_count, True), 0)[1], 0)
    lax.fori_loop(
        CHUNKS, 2 * CHUNKS, lambda t, _: (push_back(t, oth_ref, other_count, False), 0)[1], 0
    )
    for s in range(CHIPS):
        rows = pl.ds(info_ref[s], SLOTS)
        dkv_out[s, :, 0:HEAD] = dk_sum[rows, :].astype(BF16)
        dkv_out[s, :, HEAD : 2 * HEAD] = dv_sum[rows, :].astype(BF16)


def place_kernel(
    picked_ref, gate_ref, dkv_ref, dq_own, dq_peer, delta_ref, q_out, k_out, v_out, logit_out
):
    placed = place_matrix(picked_ref[...])
    scatter = placed.astype(BF16)
    total = dkv_ref[0].astype(F32)
    for s in range(1, CHIPS):
        total = total + dkv_ref[s].astype(F32)
    k_rows = (total[:, 0:HEAD] * FACTOR).astype(BF16)
    v_rows = total[:, HEAD : 2 * HEAD].astype(BF16)
    k_out[...] = jnp.dot(scatter, k_rows, preferred_element_type=F32).astype(BF16)
    v_out[...] = jnp.dot(scatter, v_rows, preferred_element_type=F32).astype(BF16)
    for h in range(GROUP):
        rows = slice(h * CHUNK, (h + 1) * CHUNK)
        parts = [
            ((dq_own[t, rows, :] + dq_peer[t, rows, :].astype(F32)) * FACTOR).astype(BF16)
            for t in range(CHUNKS)
        ]
        q_out[:, h * HEAD : (h + 1) * HEAD] = jnp.dot(
            scatter, jnp.concatenate(parts, axis=0), preferred_element_type=F32
        ).astype(BF16)
    switch = switch_of(gate_ref[...], placed)
    logit_rows = ((1.0 - switch) * delta_ref[0:1, :]).astype(BF16)
    logit_out[...] = nt_dot(logit_rows, scatter)[0:1].astype(BF16)


def whole(count):
    return [pl.BlockSpec(memory_space=pltpu.VMEM)] * count


def params():
    return pltpu.CompilerParams(vmem_limit_bytes=VMEM_BYTES)


def shape(dims, kind=BF16):
    return jax.ShapeDtypeStruct(dims, kind)


def local(head_queries, key_projection_rows, value_projection_rows, gate_logit, upstream, picked):
    picked_row = picked.reshape(1, SLOTS)
    gate_row = gate_logit.reshape(1, TOKENS)
    swap = [(0, 1), (1, 0)]
    kv_copies, qs_own = pl.pallas_call(
        pick_kernel,
        out_shape=(shape((CHIPS, SLOTS, 2 * HEAD)), shape((2, CHUNKS, ROWS, HEAD))),
        in_specs=whole(6),
        out_specs=tuple(whole(2)),
        compiler_params=params(),
        name="pick",
    )(picked_row, gate_row, key_projection_rows, value_projection_rows, head_queries, upstream)
    qs_peer = lax.ppermute(qs_own, "c", swap)
    kv_all = lax.all_to_all(kv_copies, ("y", "x"), 0, 0, tiled=True)
    kc, vc, stats, info = pl.pallas_call(
        stats_kernel,
        out_shape=(
            shape((PICKED, HEAD)),
            shape((PICKED, HEAD)),
            shape((2 * CHUNKS, 8, ROWS), F32),
            shape((32,), jnp.int32),
        ),
        in_specs=whole(3),
        out_specs=tuple(whole(3)) + (pl.BlockSpec(memory_space=pltpu.SMEM),),
        scratch_shapes=[pltpu.VMEM((PICKED + SLOTS, HEAD), F32)] * 2,
        compiler_params=params(),
        name="stats",
    )(kv_all, qs_own, qs_peer)
    stats_peer = lax.ppermute(stats, "c", swap)
    dkv, dq_own, dq_oth, deltas = pl.pallas_call(
        grad_kernel,
        out_shape=(
            shape((CHIPS, SLOTS, 2 * HEAD)),
            shape((CHUNKS, ROWS, HEAD), F32),
            shape((CHUNKS, ROWS, HEAD)),
            shape((8, SLOTS), F32),
        ),
        in_specs=[pl.BlockSpec(memory_space=pltpu.SMEM)] + whole(6),
        out_specs=tuple(whole(4)),
        scratch_shapes=[
            pltpu.VMEM((PICKED + SLOTS, HEAD), F32),
            pltpu.VMEM((PICKED + SLOTS, HEAD), F32),
            pltpu.VMEM((ROWS, HEAD), F32),
        ],
        compiler_params=params(),
        name="grads",
    )(info, kc, vc, qs_own, qs_peer, stats, stats_peer)
    dq_peer = lax.ppermute(dq_oth, "c", swap)
    delta_totals = lax.psum(deltas, "tp")
    dkv_all = lax.all_to_all(dkv, ("y", "x"), 0, 0, tiled=True)
    q_out, k_out, v_out, logit_out = pl.pallas_call(
        place_kernel,
        out_shape=(
            shape((TOKENS, GROUP * HEAD)),
            shape((TOKENS, HEAD)),
            shape((TOKENS, HEAD)),
            shape((1, TOKENS)),
        ),
        in_specs=whole(6),
        out_specs=tuple(whole(4)),
        compiler_params=params(),
        name="place",
    )(picked_row, gate_row, dkv_all, dq_own, dq_peer, delta_totals)
    return q_out, k_out, v_out, logit_out.reshape(TOKENS)


def solution(mesh):
    split = Mesh(mesh.devices.reshape(4, 4, 2, 8), ("y", "x", "c", "tp"))
    seq = ("y", "x", "c")
    return jax.shard_map(
        local,
        mesh=split,
        in_specs=(P(seq, "tp"), P(seq, "tp"), P(seq, "tp"), P(seq), P(seq, "tp"), P(seq)),
        out_specs=(P(seq, "tp"), P(seq, "tp"), P(seq, "tp"), P(seq)),
        check_vma=False,
    )
```

```python
import functools
import math

import jax
import jax.numpy as jnp
from jax import lax
from jax.experimental import pallas as pl
from jax.experimental.pallas import tpu as pltpu
from jax.sharding import Mesh, PartitionSpec as P

QUERY_HEADS = 64
KEY_VALUE_HEADS = 8
HEAD = 128
SLOTS = 128
TOKENS = 512
CHIPS = 16
PICKED = 2048
GROUP = QUERY_HEADS // KEY_VALUE_HEADS
FACTOR = 1.0 / math.sqrt(HEAD)
LOG_FACTOR = FACTOR * math.log2(math.e)
CHUNK = 32
CHUNKS = SLOTS // CHUNK
ROWS = GROUP * CHUNK
KEYS = 512
EDGE = 256
PART = 128
SPARE = 2 * CHUNKS
SENTINEL = 128.0
LIVE_BELOW = 32.0
NEGATIVE = -1e30
F32 = jnp.float32
BF16 = jnp.bfloat16
VMEM_BYTES = 48 * 1024 * 1024
VMEM_ALL = 64 * 1024 * 1024


def nt_dot(a, b):
    return lax.dot_general(a, b, (((1,), (1,)), ((), ())), preferred_element_type=F32)


def tn_dot(a, b):
    return lax.dot_general(a, b, (((0,), (0,)), ((), ())), preferred_element_type=F32)


def place_matrix(picked):
    token = lax.broadcasted_iota(jnp.int32, (TOKENS, SLOTS), 0)
    return jnp.where(token == picked, 1.0, 0.0).astype(F32)


def switch_of(gate, gather):
    rows = jnp.dot(
        jnp.broadcast_to(gate, (16, TOKENS)), gather.astype(BF16), preferred_element_type=F32
    )
    return 1.0 / (1.0 + jnp.exp(-rows))


def dead_column(picked):
    dead = jnp.where(picked >= TOKENS, SENTINEL, 0.0).astype(F32)
    return jnp.broadcast_to(dead, (SLOTS, SLOTS)).T


def fetch(pairs, sems):
    copies = [pltpu.make_async_copy(src, dst, sems.at[n]) for n, (src, dst) in enumerate(pairs)]
    for copy in copies:
        copy.start()
    for copy in copies:
        copy.wait()


def pick_kv_kernel(picked_hbm, k_hbm, v_hbm, kv_out, picked_ref, k_ref, v_ref, message, sems, out_sems):
    fetch([(picked_hbm, picked_ref), (k_hbm, k_ref), (v_hbm, v_ref)], sems)
    gather = place_matrix(picked_ref[...]).T.astype(BF16)
    keys = jnp.dot(gather, k_ref[...], preferred_element_type=F32)
    message[:, 0:HEAD] = (keys + dead_column(picked_ref[...])).astype(BF16)
    message[:, HEAD : 2 * HEAD] = jnp.dot(
        gather, v_ref[...], preferred_element_type=F32
    ).astype(BF16)
    fetch([(message, kv_out.at[chip]) for chip in range(CHIPS)], out_sems)


def pick_q_kernel(picked_hbm, gate_ref, q_hbm, up_hbm, qs_out, picked_ref, q_ref, up_ref, sems):
    fetch([(picked_hbm, picked_ref), (q_hbm, q_ref), (up_hbm, up_ref)], sems)
    placed = place_matrix(picked_ref[...])
    gather = placed.T.astype(BF16)
    switch = jnp.broadcast_to(switch_of(gate_ref[...], placed)[0:1], (SLOTS, SLOTS)).T
    for h in range(GROUP):
        lanes = slice(h * HEAD, (h + 1) * HEAD)
        q_rows = jnp.dot(gather, q_ref[:, lanes], preferred_element_type=F32).astype(BF16)
        up_rows = jnp.dot(gather, up_ref[:, lanes], preferred_element_type=F32)
        scaled = (up_rows * switch).astype(BF16)
        for t in range(CHUNKS):
            rows = slice(t * CHUNK, (t + 1) * CHUNK)
            qs_out[0, t, h * CHUNK : (h + 1) * CHUNK, :] = q_rows[rows]
            qs_out[1, t, h * CHUNK : (h + 1) * CHUNK, :] = scaled[rows]


def count_live(block):
    live = jnp.where(block.astype(F32) < LIVE_BELOW, 1.0, 0.0)
    return jnp.sum(live, axis=0, keepdims=True)[0, 0].astype(jnp.int32)


class Tiles:
    def __init__(self, core, offset, count, own_chunks, live_chunks):
        self.offset, self.count = offset, count
        self.own_chunks, self.live_chunks = own_chunks, live_chunks
        self.other_limit = offset + jnp.where(core == 0, count, 0)
        self.number = lax.div(live_chunks + 1, 2)

    def place(self, chunk):
        place = jnp.where(chunk < self.own_chunks, chunk, CHUNKS + chunk - self.own_chunks)
        return jnp.where(chunk < self.live_chunks, place, SPARE)

    def limit(self, chunk):
        slot = lax.rem(lax.broadcasted_iota(jnp.int32, (1, ROWS), 1), CHUNK)
        own = self.offset + chunk * CHUNK + 1
        step = jnp.where(chunk < self.own_chunks, 1, 0)
        return jnp.where(chunk < self.own_chunks, own, self.other_limit) + slot * step

    def bounds(self, chunk):
        own = chunk < self.own_chunks
        first = self.offset + chunk * CHUNK
        last = jnp.minimum(first + CHUNK, self.offset + self.count)
        return jnp.where(own, first + 1, self.other_limit), jnp.where(own, last, self.other_limit)

    def spans(self, tile):
        low_a, high_a = self.bounds(2 * tile)
        low_b, high_b = self.bounds(2 * tile + 1)
        paired = 2 * tile + 1 < self.live_chunks
        low = jnp.where(paired, jnp.minimum(low_a, low_b), low_a)
        high = jnp.where(paired, jnp.maximum(high_a, high_b), high_a)
        full = lax.div(low, KEYS)
        return full, lax.div(high - full * KEYS + EDGE - 1, EDGE)

    def limits(self, tile):
        return jnp.concatenate([self.limit(2 * tile), self.limit(2 * tile + 1)], axis=1)

    def sweep(self, tile, block, carry):
        full, edges = self.spans(tile)
        limits = self.limits(tile)
        start = full * KEYS
        carry = lax.fori_loop(
            0, full, lambda b, c: block(pl.multiple_of(b * KEYS, KEYS), KEYS, None, c), carry
        )
        return lax.fori_loop(
            0,
            edges,
            lambda b, c: block(pl.multiple_of(start + b * EDGE, EDGE), EDGE, limits, c),
            carry,
        )


def pair_rows(tile):
    return pl.ds(pl.multiple_of(tile * 2 * ROWS, 2 * ROWS), 2 * ROWS)


def stats_kernel(
    peer_picked, kv_ref, own_ref, oth_ref, kc_out, vc_out, q_out, s_out, stats_out, info_out,
    k_pack, v_pack,
):
    chip = lax.axis_index("y") * 4 + lax.axis_index("x")
    core = lax.axis_index("c")
    k_pack[...] = jnp.zeros_like(k_pack)
    v_pack[...] = jnp.zeros_like(v_pack)
    q_out[...] = jnp.zeros_like(q_out)
    s_out[...] = jnp.zeros_like(s_out)
    stats_out[...] = jnp.zeros_like(stats_out)
    offset = 0
    own_offset = 0
    own_count = 0
    counts = [count_live(kv_ref[s, :, 0:HEAD]) for s in range(CHIPS)]
    for s in range(CHIPS):
        k_pack[pl.ds(offset, SLOTS), :] = kv_ref[s, :, 0:HEAD].astype(F32)
        v_pack[pl.ds(offset, SLOTS), :] = kv_ref[s, :, HEAD : 2 * HEAD].astype(F32)
        info_out[s] = jnp.asarray(offset, jnp.int32)
        own_offset = jnp.where(chip == s, offset, own_offset)
        own_count = jnp.where(chip == s, counts[s], own_count)
        offset = offset + counts[s]
    peer_live = jnp.where(peer_picked[...] < TOKENS, 1.0, 0.0)
    other_count = jnp.sum(peer_live, axis=1, keepdims=True)[0, 0].astype(jnp.int32)
    own_chunks = lax.div(own_count + CHUNK - 1, CHUNK)
    live_chunks = own_chunks + lax.div(other_count + CHUNK - 1, CHUNK)
    info_out[16] = own_offset
    info_out[17] = own_count
    info_out[18] = own_chunks
    info_out[19] = live_chunks
    kc_out[...] = k_pack[0:PICKED, :].astype(BF16)
    vc_out[...] = v_pack[0:PICKED, :].astype(BF16)
    for t in range(CHUNKS):
        q_out[t * ROWS : (t + 1) * ROWS, :] = own_ref[0, t]
        s_out[t * ROWS : (t + 1) * ROWS, :] = own_ref[1, t]
    for t in range(CHUNKS):
        rows = pl.ds(pl.multiple_of((own_chunks + t) * ROWS, ROWS), ROWS)
        q_out[rows, :] = oth_ref[0, t]
        s_out[rows, :] = oth_ref[1, t]
    tiles = Tiles(core, own_offset, own_count, own_chunks, live_chunks)

    def attend(tile, _):
        q_rows = q_out[pair_rows(tile), :]
        s_rows = s_out[pair_rows(tile), :]

        def block(base, keys, limits, carry):
            top, total, pull = carry
            scores = nt_dot(kc_out[pl.ds(base, keys), :], q_rows)
            pushed = nt_dot(vc_out[pl.ds(base, keys), :], s_rows)
            for u in range(0, keys, PART):
                part = scores[u : u + PART] * LOG_FACTOR
                if limits is not None:
                    index = lax.broadcasted_iota(jnp.int32, (PART, 2 * ROWS), 0)
                    part = jnp.where(index < limits - (base + u), part, NEGATIVE)
                part = part.reshape(PART // 8, 8, 2 * ROWS)
                new_top = jnp.maximum(top, jnp.max(part, axis=0))
                raised = jnp.exp2(part - new_top[None])
                fade = jnp.exp2(top - new_top)
                total = total * fade + jnp.sum(raised, axis=0)
                pulled = raised * pushed[u : u + PART].reshape(PART // 8, 8, 2 * ROWS)
                pull = pull * fade + jnp.sum(pulled, axis=0)
                top = new_top
            return top, total, pull

        zero = jnp.zeros((8, 2 * ROWS), F32)
        top, total, pull = tiles.sweep(
            tile, block, (jnp.full((8, 2 * ROWS), NEGATIVE, F32), zero, zero)
        )
        best = jnp.max(top, axis=0, keepdims=True)
        fade = jnp.exp2(top - best)
        total = jnp.sum(total * fade, axis=0, keepdims=True)
        pull = jnp.sum(pull * fade, axis=0, keepdims=True)
        for half in range(2):
            place = tiles.place(2 * tile + half)
            lanes = slice(half * ROWS, (half + 1) * ROWS)
            stats_out[place, 0:1, :] = best[:, lanes]
            stats_out[place, 1:2, :] = total[:, lanes]
            stats_out[place, 2:3, :] = pull[:, lanes]
        return 0

    lax.fori_loop(0, tiles.number, attend, 0)


def combine_kernel(info_ref, stats_ref, peer_ref, comb_out, delta_out):
    own_chunks = info_ref[18]
    lane = lax.div(lax.broadcasted_iota(jnp.int32, (1, SLOTS), 1), CHUNK)
    comb_out[SPARE] = jnp.zeros((8, ROWS), F32)
    deltas = jnp.zeros((1, SLOTS), F32)
    for place in range(SPARE):
        mine = stats_ref[place]
        theirs = peer_ref[(place + CHUNKS) % SPARE]
        top = jnp.maximum(mine[0:1], theirs[0:1])
        mine_scale = jnp.exp2(mine[0:1] - top)
        their_scale = jnp.exp2(theirs[0:1] - top)
        total = mine[1:2] * mine_scale + theirs[1:2] * their_scale
        total = jnp.where(total > 0.0, total, 1.0)
        delta = (mine[2:3] * mine_scale + theirs[2:3] * their_scale) / total
        comb_out[place, 0:1, :] = top + jnp.log2(total)
        comb_out[place, 1:2, :] = delta
        if place < CHUNKS:
            heads = delta[:, 0:128] + delta[:, 128:256]
            heads = heads + pltpu.roll(heads, 64, 1)
            heads = heads + pltpu.roll(heads, 32, 1)
            mark = jnp.where(place < own_chunks, place, CHUNKS)
            deltas = deltas + jnp.where(lane == mark, heads, 0.0)
    delta_out[...] = jnp.broadcast_to(deltas, (8, SLOTS))


def grad_kernel(
    info_ref, kc_ref, vc_ref, q_ref, s_ref, comb_ref, dkv_out, dq_own, dq_oth,
    dk_sum, dv_sum, dq_sum,
):
    core = lax.axis_index("c")
    tiles = Tiles(core, info_ref[16], info_ref[17], info_ref[18], info_ref[19])
    dk_sum[...] = jnp.zeros_like(dk_sum)
    dv_sum[...] = jnp.zeros_like(dv_sum)
    dq_own[...] = jnp.zeros_like(dq_own)
    dq_oth[...] = jnp.zeros_like(dq_oth)

    def push_back(tile, _):
        q_rows = q_ref[pair_rows(tile), :]
        s_rows = s_ref[pair_rows(tile), :]
        chunks = (2 * tile, 2 * tile + 1)
        comb = jnp.concatenate([comb_ref[tiles.place(c)] for c in chunks], axis=1)
        level, delta = comb[0:1], comb[1:2]
        dq_sum[...] = jnp.zeros_like(dq_sum)

        def block(base, keys, limits, carry):
            span = pl.ds(base, keys)
            key_rows = kc_ref[span, :]
            scores = nt_dot(key_rows, q_rows)
            pushed = nt_dot(vc_ref[span, :], s_rows)
            weights = jnp.exp2(scores * LOG_FACTOR - level)
            if limits is not None:
                index = lax.broadcasted_iota(jnp.int32, (keys, 2 * ROWS), 0)
                weights = jnp.where(index < limits - base, weights, 0.0)
            slopes = (weights * (pushed - delta)).astype(BF16)
            dv_sum[span, :] += jnp.dot(
                weights.astype(BF16), s_rows, preferred_element_type=F32
            )
            dk_sum[span, :] += jnp.dot(slopes, q_rows, preferred_element_type=F32)
            dq_sum[...] += tn_dot(slopes, key_rows)
            return carry

        tiles.sweep(tile, block, 0)
        for half, chunk in enumerate(chunks):
            rows = slice(half * ROWS, (half + 1) * ROWS)

            @pl.when(chunk < tiles.own_chunks)
            def _():
                dq_own[chunk] = dq_sum[rows, :]

            @pl.when((chunk >= tiles.own_chunks) & (chunk < tiles.live_chunks))
            def _():
                dq_oth[chunk - tiles.own_chunks] = dq_sum[rows, :].astype(BF16)

        return 0

    lax.fori_loop(0, tiles.number, push_back, 0)
    for s in range(CHIPS):
        rows = pl.ds(info_ref[s], SLOTS)
        dkv_out[s, :, 0:HEAD] = dk_sum[rows, :].astype(BF16)
        dkv_out[s, :, HEAD : 2 * HEAD] = dv_sum[rows, :].astype(BF16)


def place_q_kernel(picked_ref, gate_ref, dq_own, dq_peer, q_out, closed_out):
    placed = place_matrix(picked_ref[...])
    scatter = placed.astype(BF16)
    closed_out[...] = 1.0 - switch_of(gate_ref[...], placed)
    for h in range(GROUP):
        rows = slice(h * CHUNK, (h + 1) * CHUNK)
        parts = [
            ((dq_own[t, rows, :] + dq_peer[t, rows, :].astype(F32)) * FACTOR).astype(BF16)
            for t in range(CHUNKS)
        ]
        q_out[:, h * HEAD : (h + 1) * HEAD] = jnp.dot(
            scatter, jnp.concatenate(parts, axis=0), preferred_element_type=F32
        ).astype(BF16)


def place_logit_kernel(picked_ref, closed_ref, delta_half, delta_rest, logit_out):
    scatter = place_matrix(picked_ref[...]).astype(BF16)
    deltas = delta_half[0:1, :] + delta_rest[0:1, :]
    logit_rows = (closed_ref[...] * deltas).astype(BF16)
    logit_out[...] = nt_dot(logit_rows, scatter)[0:1].astype(BF16)


def place_kv_kernel(picked_ref, dkv_ref, k_out, v_out):
    scatter = place_matrix(picked_ref[...]).astype(BF16)
    total = dkv_ref[0].astype(F32)
    for s in range(1, CHIPS):
        total = total + dkv_ref[s].astype(F32)
    k_rows = (total[:, 0:HEAD] * FACTOR).astype(BF16)
    v_rows = total[:, HEAD : 2 * HEAD].astype(BF16)
    k_out[...] = jnp.dot(scatter, k_rows, preferred_element_type=F32).astype(BF16)
    v_out[...] = jnp.dot(scatter, v_rows, preferred_element_type=F32).astype(BF16)


def whole(count):
    return [pl.BlockSpec(memory_space=pltpu.VMEM)] * count


def params(limit=VMEM_BYTES):
    return pltpu.CompilerParams(vmem_limit_bytes=limit)


def shape(dims, kind=BF16):
    return jax.ShapeDtypeStruct(dims, kind)


def hbm(count):
    return [pl.BlockSpec(memory_space=pltpu.HBM)] * count


def cost(flops):
    return pl.CostEstimate(flops=flops, bytes_accessed=1 << 20, transcendentals=0)


def local(head_queries, key_projection_rows, value_projection_rows, gate_logit, upstream, picked):
    picked_row = picked.reshape(1, SLOTS)
    swap = [(0, 1), (1, 0)]
    kv_copies = pl.pallas_call(
        pick_kv_kernel,
        out_shape=shape((CHIPS, SLOTS, 2 * HEAD)),
        in_specs=hbm(3),
        out_specs=hbm(1)[0],
        scratch_shapes=[
            pltpu.VMEM((1, SLOTS), jnp.int32),
            pltpu.VMEM((TOKENS, HEAD), BF16),
            pltpu.VMEM((TOKENS, HEAD), BF16),
            pltpu.VMEM((SLOTS, 2 * HEAD), BF16),
            pltpu.SemaphoreType.DMA((3,)),
            pltpu.SemaphoreType.DMA((CHIPS,)),
        ],
        compiler_params=params(VMEM_ALL),
        name="pick_kv",
    )(picked_row, key_projection_rows, value_projection_rows)
    kv_all = lax.all_to_all(kv_copies, ("y", "x"), 0, 0, tiled=True)
    gate_row = gate_logit.reshape(1, TOKENS)
    qs_own = pl.pallas_call(
        pick_q_kernel,
        out_shape=shape((2, CHUNKS, ROWS, HEAD)),
        in_specs=hbm(1) + whole(1) + hbm(2),
        out_specs=whole(1)[0],
        scratch_shapes=[
            pltpu.VMEM((1, SLOTS), jnp.int32),
            pltpu.VMEM((TOKENS, GROUP * HEAD), BF16),
            pltpu.VMEM((TOKENS, GROUP * HEAD), BF16),
            pltpu.SemaphoreType.DMA((3,)),
        ],
        compiler_params=params(),
        cost_estimate=cost(1 << 30),
        name="pick_q",
    )(picked_row, gate_row, head_queries, upstream)
    qs_peer = lax.ppermute(qs_own, "c", swap)
    peer_picked = lax.ppermute(picked_row, "c", swap)
    kc, vc, q_rows, s_rows, stats, info = pl.pallas_call(
        stats_kernel,
        out_shape=(
            shape((PICKED, HEAD)),
            shape((PICKED, HEAD)),
            shape((2 * CHUNKS * ROWS, HEAD)),
            shape((2 * CHUNKS * ROWS, HEAD)),
            shape((SPARE + 1, 8, ROWS), F32),
            shape((32,), jnp.int32),
        ),
        in_specs=whole(4),
        out_specs=tuple(whole(5)) + (pl.BlockSpec(memory_space=pltpu.SMEM),),
        scratch_shapes=[pltpu.VMEM((PICKED + SLOTS, HEAD), F32)] * 2,
        compiler_params=params(),
        name="stats",
    )(peer_picked, kv_all, qs_own, qs_peer)
    stats_peer = lax.ppermute(stats, "c", swap)
    comb, deltas = pl.pallas_call(
        combine_kernel,
        out_shape=(shape((SPARE + 1, 8, ROWS), F32), shape((8, SLOTS), F32)),
        in_specs=[pl.BlockSpec(memory_space=pltpu.SMEM)] + whole(2),
        out_specs=tuple(whole(2)),
        compiler_params=params(),
        name="combine",
    )(info, stats, stats_peer)
    delta_near = lax.ppermute(deltas, "tp", [(i, i ^ 1) for i in range(8)])
    dkv, dq_own, dq_oth = pl.pallas_call(
        grad_kernel,
        out_shape=(
            shape((CHIPS, SLOTS, 2 * HEAD)),
            shape((CHUNKS, ROWS, HEAD), F32),
            shape((CHUNKS, ROWS, HEAD)),
        ),
        in_specs=[pl.BlockSpec(memory_space=pltpu.SMEM)] + whole(5),
        out_specs=tuple(whole(3)),
        scratch_shapes=[
            pltpu.VMEM((PICKED + SLOTS, HEAD), F32),
            pltpu.VMEM((PICKED + SLOTS, HEAD), F32),
            pltpu.VMEM((2 * ROWS, HEAD), F32),
        ],
        compiler_params=params(),
        cost_estimate=cost(1 << 32),
        name="grads",
    )(info, kc, vc, q_rows, s_rows, comb)
    dkv, delta_near = lax.optimization_barrier((dkv, delta_near))
    dkv_all = lax.all_to_all(dkv, ("y", "x"), 0, 0, tiled=True)
    delta_pair = deltas + delta_near
    delta_half = delta_pair + lax.ppermute(delta_pair, "tp", [(i, i ^ 2) for i in range(8)])
    delta_rest = lax.ppermute(delta_half, "tp", [(i, i ^ 4) for i in range(8)])
    dq_peer = lax.ppermute(dq_oth, "c", swap)
    q_out, closed = pl.pallas_call(
        place_q_kernel,
        out_shape=(shape((TOKENS, GROUP * HEAD)), shape((16, SLOTS), F32)),
        in_specs=whole(4),
        out_specs=tuple(whole(2)),
        compiler_params=params(),
        cost_estimate=cost(1 << 29),
        name="place_q",
    )(picked_row, gate_row, dq_own, dq_peer)
    logit_out = pl.pallas_call(
        place_logit_kernel,
        out_shape=shape((1, TOKENS)),
        in_specs=whole(4),
        out_specs=whole(1)[0],
        compiler_params=params(),
        cost_estimate=cost(1 << 28),
        name="place_logit",
    )(picked_row, closed, delta_half, delta_rest)
    k_out, v_out = pl.pallas_call(
        place_kv_kernel,
        out_shape=(shape((TOKENS, HEAD)), shape((TOKENS, HEAD))),
        in_specs=whole(2),
        out_specs=tuple(whole(2)),
        compiler_params=params(),
        name="place_kv",
    )(picked_row, dkv_all)
    return q_out, k_out, v_out, logit_out.reshape(TOKENS)


def solution(mesh):
    split = Mesh(mesh.devices.reshape(4, 4, 2, 8), ("y", "x", "c", "tp"))
    seq = ("y", "x", "c")
    return jax.shard_map(
        local,
        mesh=split,
        in_specs=(P(seq, "tp"), P(seq, "tp"), P(seq, "tp"), P(seq), P(seq, "tp"), P(seq)),
        out_specs=(P(seq, "tp"), P(seq, "tp"), P(seq, "tp"), P(seq)),
        check_vma=False,
    )
```

```python
import functools
import math

import jax
import jax.numpy as jnp
from jax import lax
from jax.experimental import pallas as pl
from jax.experimental.pallas import tpu as pltpu
from jax.sharding import Mesh, PartitionSpec as P

QUERY_HEADS = 64
KEY_VALUE_HEADS = 8
HEAD = 128
SLOTS = 128
TOKENS = 512
CHIPS = 16
PICKED = 2048
GROUP = QUERY_HEADS // KEY_VALUE_HEADS
FACTOR = 1.0 / math.sqrt(HEAD)
LOG_FACTOR = FACTOR * math.log2(math.e)
CHUNK = 32
CHUNKS = SLOTS // CHUNK
ROWS = GROUP * CHUNK
KEYS = 512
EDGE = 256
PART = 128
SPARE = 2 * CHUNKS
KEPT = 1536
KERNEL_BYTES = 16 * 1024 * 1024
SENTINEL = 128.0
LIVE_BELOW = 32.0
NEGATIVE = -1e30
F32 = jnp.float32
BF16 = jnp.bfloat16
VMEM_BYTES = 48 * 1024 * 1024
VMEM_ALL = 64 * 1024 * 1024


def nt_dot(a, b):
    return lax.dot_general(a, b, (((1,), (1,)), ((), ())), preferred_element_type=F32)


def tn_dot(a, b):
    return lax.dot_general(a, b, (((0,), (0,)), ((), ())), preferred_element_type=F32)


def place_matrix(picked):
    token = lax.broadcasted_iota(jnp.int32, (TOKENS, SLOTS), 0)
    return jnp.where(token == picked, 1.0, 0.0).astype(F32)


def switch_of(gate, gather):
    rows = jnp.dot(
        jnp.broadcast_to(gate, (16, TOKENS)), gather.astype(BF16), preferred_element_type=F32
    )
    return 1.0 / (1.0 + jnp.exp(-rows))


def fetch(pairs, sems):
    copies = [pltpu.make_async_copy(src, dst, sems.at[n]) for n, (src, dst) in enumerate(pairs)]
    for copy in copies:
        copy.start()
    for copy in copies:
        copy.wait()


def pick_kv_kernel(picked_hbm, k_hbm, v_hbm, kv_out, picked_ref, k_ref, v_ref, message, sems, out_sems):
    pairs = [(picked_hbm, picked_ref), (k_hbm, k_ref), (v_hbm, v_ref)]
    copies = [pltpu.make_async_copy(src, dst, sems.at[n]) for n, (src, dst) in enumerate(pairs)]
    for copy in copies:
        copy.start()
    copies[0].wait()
    column = jnp.broadcast_to(picked_ref[...], (SLOTS, SLOTS)).astype(F32).T
    token = lax.broadcasted_iota(jnp.int32, (SLOTS, SLOTS), 1).astype(F32)
    gather = jnp.concatenate(
        [jnp.where(token + base == column, 1.0, 0.0) for base in range(0, TOKENS, SLOTS)], axis=1
    ).astype(BF16)
    dead = jnp.where(column >= TOKENS, SENTINEL, 0.0)
    copies[1].wait()
    keys = jnp.dot(gather, k_ref[...], preferred_element_type=F32)
    message[:, 0:HEAD] = (keys + dead).astype(BF16)
    copies[2].wait()
    message[:, HEAD : 2 * HEAD] = jnp.dot(
        gather, v_ref[...], preferred_element_type=F32
    ).astype(BF16)
    fetch([(message, kv_out.at[chip]) for chip in range(CHIPS)], out_sems)


def pick_q_kernel(picked_hbm, gate_ref, q_hbm, up_hbm, qs_out, picked_ref, q_ref, up_ref, sems):
    fetch([(picked_hbm, picked_ref), (q_hbm, q_ref), (up_hbm, up_ref)], sems)
    placed = place_matrix(picked_ref[...])
    gather = placed.T.astype(BF16)
    switch = jnp.broadcast_to(switch_of(gate_ref[...], placed)[0:1], (SLOTS, SLOTS)).T
    for h in range(GROUP):
        lanes = slice(h * HEAD, (h + 1) * HEAD)
        q_rows = jnp.dot(gather, q_ref[:, lanes], preferred_element_type=F32).astype(BF16)
        up_rows = jnp.dot(gather, up_ref[:, lanes], preferred_element_type=F32)
        scaled = (up_rows * switch).astype(BF16)
        for t in range(CHUNKS):
            rows = slice(t * CHUNK, (t + 1) * CHUNK)
            qs_out[0, t, h * CHUNK : (h + 1) * CHUNK, :] = q_rows[rows]
            qs_out[1, t, h * CHUNK : (h + 1) * CHUNK, :] = scaled[rows]


def count_live(block):
    live = jnp.where(block.astype(F32) < LIVE_BELOW, 1.0, 0.0)
    return jnp.sum(live, axis=0, keepdims=True)[0, 0].astype(jnp.int32)


class Tiles:
    def __init__(self, core, offset, count, own_chunks, live_chunks):
        self.offset, self.count = offset, count
        self.own_chunks, self.live_chunks = own_chunks, live_chunks
        self.other_limit = offset + jnp.where(core == 0, count, 0)
        self.number = lax.div(live_chunks + 1, 2)

    def place(self, chunk):
        place = jnp.where(chunk < self.own_chunks, chunk, CHUNKS + chunk - self.own_chunks)
        return jnp.where(chunk < self.live_chunks, place, SPARE)

    def peer_place(self, chunk):
        place = self.place(chunk)
        return jnp.where(place == SPARE, SPARE, lax.rem(place + CHUNKS, 2 * CHUNKS))

    def limit(self, chunk):
        slot = lax.rem(lax.broadcasted_iota(jnp.int32, (1, ROWS), 1), CHUNK)
        own = self.offset + chunk * CHUNK + 1
        step = jnp.where(chunk < self.own_chunks, 1, 0)
        return jnp.where(chunk < self.own_chunks, own, self.other_limit) + slot * step

    def bounds(self, chunk):
        own = chunk < self.own_chunks
        first = self.offset + chunk * CHUNK
        last = jnp.minimum(first + CHUNK, self.offset + self.count)
        return jnp.where(own, first + 1, self.other_limit), jnp.where(own, last, self.other_limit)

    def spans(self, tile):
        low_a, high_a = self.bounds(2 * tile)
        low_b, high_b = self.bounds(2 * tile + 1)
        paired = 2 * tile + 1 < self.live_chunks
        low = jnp.where(paired, jnp.minimum(low_a, low_b), low_a)
        high = jnp.where(paired, jnp.maximum(high_a, high_b), high_a)
        full = lax.div(low, KEYS)
        rest = high - full * KEYS
        wide = lax.div(rest + EDGE - 1, KEYS)
        return full, wide, rest > wide * KEYS

    def limits(self, tile):
        return jnp.concatenate([self.limit(2 * tile), self.limit(2 * tile + 1)], axis=1)

    def sweep(self, tile, block, carry):
        full, wide, narrow = self.spans(tile)
        limits = self.limits(tile)

        def run(first, count, keys, limits, carry):
            def steps(kept):
                return lambda b, carry: block(
                    pl.multiple_of(first + b * keys, keys), keys, limits, kept, carry
                )

            inside = jnp.minimum(jnp.maximum(lax.div(KEPT - first, keys), 0), count)
            carry = lax.fori_loop(0, inside, steps(True), carry)
            return lax.fori_loop(inside, count, steps(False), carry)

        carry = run(0, full, KEYS, None, carry)
        carry = run(full * KEYS, wide, KEYS, limits, carry)
        last = (full + wide) * KEYS
        return run(last, jnp.where(narrow, 1, 0), EDGE, limits, carry)


def pair_rows(tile):
    return pl.ds(pl.multiple_of(tile * 2 * ROWS, 2 * ROWS), 2 * ROWS)


def stats_kernel(
    peer_picked, kv_ref, own_ref, oth_ref, kc_out, vc_out, q_out, s_out, stats_out, scores_out,
    pushed_out, info_out, k_pack, v_pack,
):
    chip = lax.axis_index("y") * 4 + lax.axis_index("x")
    core = lax.axis_index("c")
    stats_out[...] = jnp.zeros_like(stats_out)
    offset = 0
    own_offset = 0
    own_count = 0
    counts = [count_live(kv_ref[s, :, 0:HEAD]) for s in range(CHIPS)]
    for s in range(CHIPS):
        k_pack[pl.ds(offset, SLOTS), :] = kv_ref[s, :, 0:HEAD].astype(F32)
        v_pack[pl.ds(offset, SLOTS), :] = kv_ref[s, :, HEAD : 2 * HEAD].astype(F32)
        info_out[s] = jnp.asarray(offset, jnp.int32)
        own_offset = jnp.where(chip == s, offset, own_offset)
        own_count = jnp.where(chip == s, counts[s], own_count)
        offset = offset + counts[s]
    peer_live = jnp.where(peer_picked[...] < TOKENS, 1.0, 0.0)
    other_count = jnp.sum(peer_live, axis=1, keepdims=True)[0, 0].astype(jnp.int32)
    own_chunks = lax.div(own_count + CHUNK - 1, CHUNK)
    live_chunks = own_chunks + lax.div(other_count + CHUNK - 1, CHUNK)
    info_out[16] = own_offset
    info_out[17] = own_count
    info_out[18] = own_chunks
    info_out[19] = live_chunks
    tail = pl.ds(offset + SLOTS, KEYS)
    k_pack[tail, :] = jnp.zeros((KEYS, HEAD), F32)
    v_pack[tail, :] = jnp.zeros((KEYS, HEAD), F32)

    def narrow_keys(b, _):
        rows = pl.ds(pl.multiple_of(b * KEYS, KEYS), KEYS)
        kc_out[rows, :] = k_pack[rows, :].astype(BF16)
        vc_out[rows, :] = v_pack[rows, :].astype(BF16)
        return 0

    lax.fori_loop(0, lax.div(own_offset + own_count + KEYS - 1, KEYS), narrow_keys, 0)
    for t in range(CHUNKS):
        q_out[t * ROWS : (t + 1) * ROWS, :] = own_ref[0, t]
        s_out[t * ROWS : (t + 1) * ROWS, :] = own_ref[1, t]
    for t in range(CHUNKS):
        rows = pl.ds(pl.multiple_of((own_chunks + t) * ROWS, ROWS), ROWS)
        q_out[rows, :] = oth_ref[0, t]
        s_out[rows, :] = oth_ref[1, t]
    spare = pl.ds(pl.multiple_of(live_chunks * ROWS, ROWS), ROWS)
    q_out[spare, :] = jnp.zeros((ROWS, HEAD), BF16)
    s_out[spare, :] = jnp.zeros((ROWS, HEAD), BF16)
    tiles = Tiles(core, own_offset, own_count, own_chunks, live_chunks)

    def attend(tile, _):
        q_rows = q_out[pair_rows(tile), :]
        s_rows = s_out[pair_rows(tile), :]

        def block(base, keys, limits, kept, carry):
            top, total, pull = carry
            scores = nt_dot(kc_out[pl.ds(base, keys), :], q_rows)
            pushed = nt_dot(vc_out[pl.ds(base, keys), :], s_rows)
            if kept:
                scores_out[tile, pl.ds(base, keys), :] = scores
                pushed_out[tile, pl.ds(base, keys), :] = pushed
            for u in range(0, keys, PART):
                part = scores[u : u + PART] * LOG_FACTOR
                if limits is not None:
                    index = lax.broadcasted_iota(jnp.int32, (PART, 2 * ROWS), 0)
                    part = jnp.where(index < limits - (base + u), part, NEGATIVE)
                part = part.reshape(PART // 8, 8, 2 * ROWS)
                new_top = jnp.maximum(top, jnp.max(part, axis=0))
                raised = jnp.exp2(part - new_top[None])
                fade = jnp.exp2(top - new_top)
                total = total * fade + jnp.sum(raised, axis=0)
                pulled = raised * pushed[u : u + PART].reshape(PART // 8, 8, 2 * ROWS)
                pull = pull * fade + jnp.sum(pulled, axis=0)
                top = new_top
            return top, total, pull

        zero = jnp.zeros((8, 2 * ROWS), F32)
        top, total, pull = tiles.sweep(
            tile, block, (jnp.full((8, 2 * ROWS), NEGATIVE, F32), zero, zero)
        )
        best = jnp.max(top, axis=0, keepdims=True)
        fade = jnp.exp2(top - best)
        total = jnp.sum(total * fade, axis=0, keepdims=True)
        pull = jnp.sum(pull * fade, axis=0, keepdims=True)
        for half in range(2):
            place = tiles.place(2 * tile + half)
            lanes = slice(half * ROWS, (half + 1) * ROWS)
            stats_out[place, 0:1, :] = best[:, lanes]
            stats_out[place, 1:2, :] = total[:, lanes]
            stats_out[place, 2:3, :] = pull[:, lanes]
        return 0

    lax.fori_loop(0, tiles.number, attend, 0)


def grad_kernel(
    info_ref, kc_ref, vc_ref, q_ref, s_ref, stats_ref, peer_ref, scores_ref, pushed_ref, dkv_out, dq_own, dq_oth, delta_out,
    dk_sum, dv_sum, dq_sum, message, sems,
):
    core = lax.axis_index("c")
    tiles = Tiles(core, info_ref[16], info_ref[17], info_ref[18], info_ref[19])
    dk_sum[...] = jnp.zeros_like(dk_sum)
    dv_sum[...] = jnp.zeros_like(dv_sum)
    dq_own[...] = jnp.zeros_like(dq_own)
    dq_oth[...] = jnp.zeros_like(dq_oth)
    delta_out[...] = jnp.zeros_like(delta_out)

    def push_back(tile, _):
        q_rows = q_ref[pair_rows(tile), :]
        s_rows = s_ref[pair_rows(tile), :]
        chunks = (2 * tile, 2 * tile + 1)
        mine = jnp.concatenate([stats_ref[tiles.place(c)] for c in chunks], axis=1)
        theirs = jnp.concatenate([peer_ref[tiles.peer_place(c)] for c in chunks], axis=1)
        top = jnp.maximum(mine[0:1], theirs[0:1])
        mine_scale = jnp.exp2(mine[0:1] - top)
        their_scale = jnp.exp2(theirs[0:1] - top)
        total = mine[1:2] * mine_scale + theirs[1:2] * their_scale
        total = jnp.where(total > 0.0, total, 1.0)
        delta = (mine[2:3] * mine_scale + theirs[2:3] * their_scale) / total
        level = top + jnp.log2(total)
        lane = lax.div(lax.broadcasted_iota(jnp.int32, (1, SLOTS), 1), CHUNK)
        for half, chunk in enumerate(chunks):
            first = half * ROWS
            heads = delta[:, first : first + 128] + delta[:, first + 128 : first + 256]
            heads = heads + pltpu.roll(heads, 64, 1)
            heads = heads + pltpu.roll(heads, 32, 1)
            mark = jnp.where(chunk < tiles.own_chunks, chunk, CHUNKS)
            delta_out[0:1, :] += jnp.where(lane == mark, heads, 0.0)
        dq_sum[...] = jnp.zeros_like(dq_sum)

        def block(base, keys, limits, kept, carry):
            span = pl.ds(base, keys)
            key_rows = kc_ref[span, :]
            if kept:
                scores = scores_ref[tile, span, :]
                pushed = pushed_ref[tile, span, :]
            else:
                scores = nt_dot(key_rows, q_rows)
                pushed = nt_dot(vc_ref[span, :], s_rows)
            weights = jnp.exp2(scores * LOG_FACTOR - level)
            if limits is not None:
                index = lax.broadcasted_iota(jnp.int32, (keys, 2 * ROWS), 0)
                weights = jnp.where(index < limits - base, weights, 0.0)
            slopes = (weights * (pushed - delta)).astype(BF16)
            dv_sum[span, :] += jnp.dot(
                weights.astype(BF16), s_rows, preferred_element_type=F32
            )
            dk_sum[span, :] += jnp.dot(slopes, q_rows, preferred_element_type=F32)
            dq_sum[...] += tn_dot(slopes, key_rows)
            return carry

        tiles.sweep(tile, block, 0)
        for half, chunk in enumerate(chunks):
            rows = slice(half * ROWS, (half + 1) * ROWS)

            @pl.when(chunk < tiles.own_chunks)
            def _():
                dq_own[chunk] = dq_sum[rows, :]

            @pl.when((chunk >= tiles.own_chunks) & (chunk < tiles.live_chunks))
            def _():
                dq_oth[chunk - tiles.own_chunks] = dq_sum[rows, :].astype(BF16)

        return 0

    lax.fori_loop(0, tiles.number, push_back, 0)
    copies = []
    for s in range(CHIPS):
        rows = pl.ds(info_ref[s], SLOTS)
        message[s, :, 0:HEAD] = dk_sum[rows, :].astype(BF16)
        message[s, :, HEAD : 2 * HEAD] = dv_sum[rows, :].astype(BF16)
        copies.append(pltpu.make_async_copy(message.at[s], dkv_out.at[(s % 4) * 4 + s // 4], sems.at[s]))
        copies[s].start()
    for copy in copies:
        copy.wait()


def place_q_kernel(picked_ref, gate_ref, dq_own, dq_peer, q_out, closed_out):
    placed = place_matrix(picked_ref[...])
    scatter = placed.astype(BF16)
    closed_out[...] = 1.0 - switch_of(gate_ref[...], placed)
    for h in range(GROUP):
        rows = slice(h * CHUNK, (h + 1) * CHUNK)
        parts = [
            ((dq_own[t, rows, :] + dq_peer[t, rows, :].astype(F32)) * FACTOR).astype(BF16)
            for t in range(CHUNKS)
        ]
        q_out[:, h * HEAD : (h + 1) * HEAD] = jnp.dot(
            scatter, jnp.concatenate(parts, axis=0), preferred_element_type=F32
        ).astype(BF16)


def place_logit_kernel(picked_ref, closed_ref, delta_a, delta_b, delta_c, delta_d, logit_out):
    scatter = place_matrix(picked_ref[...]).astype(BF16)
    deltas = (delta_a[0:1, :] + delta_b[0:1, :]) + (delta_c[0:1, :] + delta_d[0:1, :])
    logit_rows = (closed_ref[...] * deltas).astype(BF16)
    for part in range(TOKENS // SLOTS):
        rows = slice(part * SLOTS, (part + 1) * SLOTS)
        logit_out[part : part + 1, :] = nt_dot(logit_rows, scatter[rows])[0:1].astype(BF16)


def place_kv_kernel(picked_ref, dkv_ref, k_out, v_out):
    scatter = place_matrix(picked_ref[...]).astype(BF16)
    total = dkv_ref[0].astype(F32)
    for s in range(1, CHIPS):
        total = total + dkv_ref[s].astype(F32)
    k_rows = (total[:, 0:HEAD] * FACTOR).astype(BF16)
    v_rows = total[:, HEAD : 2 * HEAD].astype(BF16)
    k_out[...] = jnp.dot(scatter, k_rows, preferred_element_type=F32).astype(BF16)
    v_out[...] = jnp.dot(scatter, v_rows, preferred_element_type=F32).astype(BF16)


def whole(count):
    return [pl.BlockSpec(memory_space=pltpu.VMEM)] * count


def params(limit=VMEM_BYTES):
    return pltpu.CompilerParams(vmem_limit_bytes=limit)


def shape(dims, kind=BF16):
    return jax.ShapeDtypeStruct(dims, kind)


def hbm(count):
    return [pl.BlockSpec(memory_space=pltpu.HBM)] * count


def cost(flops):
    return pl.CostEstimate(flops=flops, bytes_accessed=1 << 20, transcendentals=0)


def local(head_queries, key_projection_rows, value_projection_rows, gate_logit, upstream, picked):
    picked_row = picked.reshape(1, SLOTS)
    swap = [(0, 1), (1, 0)]
    kv_copies = pl.pallas_call(
        pick_kv_kernel,
        out_shape=shape((CHIPS, SLOTS, 2 * HEAD)),
        in_specs=hbm(3),
        out_specs=hbm(1)[0],
        scratch_shapes=[
            pltpu.VMEM((1, SLOTS), jnp.int32),
            pltpu.VMEM((TOKENS, HEAD), BF16),
            pltpu.VMEM((TOKENS, HEAD), BF16),
            pltpu.VMEM((SLOTS, 2 * HEAD), BF16),
            pltpu.SemaphoreType.DMA((3,)),
            pltpu.SemaphoreType.DMA((CHIPS,)),
        ],
        compiler_params=params(VMEM_ALL),
        name="pick_kv",
    )(picked_row, key_projection_rows, value_projection_rows)
    kv_all = lax.all_to_all(kv_copies, ("y", "x"), 0, 0, tiled=True)
    gate_row = gate_logit.reshape(1, TOKENS)
    qs_own = pl.pallas_call(
        pick_q_kernel,
        out_shape=shape((2, CHUNKS, ROWS, HEAD)),
        in_specs=hbm(1) + whole(1) + hbm(2),
        out_specs=whole(1)[0],
        scratch_shapes=[
            pltpu.VMEM((1, SLOTS), jnp.int32),
            pltpu.VMEM((TOKENS, GROUP * HEAD), BF16),
            pltpu.VMEM((TOKENS, GROUP * HEAD), BF16),
            pltpu.SemaphoreType.DMA((3,)),
        ],
        compiler_params=params(),
        cost_estimate=cost(1 << 30),
        name="pick_q",
    )(picked_row, gate_row, head_queries, upstream)
    qs_peer = lax.ppermute(qs_own, "c", swap)
    peer_picked = lax.ppermute(picked_row, "c", swap)
    kc, vc, q_rows, s_rows, stats, scores, pushed, info = pl.pallas_call(
        stats_kernel,
        out_shape=(
            shape((PICKED, HEAD)),
            shape((PICKED, HEAD)),
            shape(((2 * CHUNKS + 1) * ROWS, HEAD)),
            shape(((2 * CHUNKS + 1) * ROWS, HEAD)),
            shape((SPARE + 1, 8, ROWS), F32),
            shape((CHUNKS, KEPT, 2 * ROWS), F32),
            shape((CHUNKS, KEPT, 2 * ROWS), F32),
            shape((32,), jnp.int32),
        ),
        in_specs=whole(4),
        out_specs=tuple(whole(7)) + (pl.BlockSpec(memory_space=pltpu.SMEM),),
        scratch_shapes=[pltpu.VMEM((PICKED + SLOTS + KEYS, HEAD), F32)] * 2,
        compiler_params=params(KERNEL_BYTES),
        name="stats",
    )(peer_picked, kv_all, qs_own, qs_peer)
    stats_peer = lax.ppermute(stats, "c", swap)
    dkv, dq_own, dq_oth, deltas = pl.pallas_call(
        grad_kernel,
        out_shape=(
            shape((CHIPS, SLOTS, 2 * HEAD)),
            shape((CHUNKS, ROWS, HEAD), F32),
            shape((CHUNKS, ROWS, HEAD)),
            shape((8, SLOTS), F32),
        ),
        in_specs=[pl.BlockSpec(memory_space=pltpu.SMEM)] + whole(8),
        out_specs=tuple(hbm(1) + whole(3)),
        scratch_shapes=[
            pltpu.VMEM((PICKED + SLOTS, HEAD), F32),
            pltpu.VMEM((PICKED + SLOTS, HEAD), F32),
            pltpu.VMEM((2 * ROWS, HEAD), F32),
            pltpu.VMEM((CHIPS, SLOTS, 2 * HEAD), BF16),
            pltpu.SemaphoreType.DMA((CHIPS,)),
        ],
        compiler_params=params(KERNEL_BYTES),
        cost_estimate=cost(1 << 32),
        name="grads",
    )(info, kc, vc, q_rows, s_rows, stats, stats_peer, scores, pushed)
    dkv_all = lax.all_to_all(dkv, ("x", "y"), 0, 0, tiled=True)
    delta_half = deltas + lax.ppermute(deltas, "tp", [(i, i ^ 4) for i in range(8)])
    delta_parts = [delta_half] + [
        lax.ppermute(delta_half, "tp", [(i, i ^ k) for i in range(8)]) for k in (1, 2, 3)
    ]
    dq_peer = lax.ppermute(dq_oth, "c", swap)
    q_out, closed = pl.pallas_call(
        place_q_kernel,
        out_shape=(shape((TOKENS, GROUP * HEAD)), shape((16, SLOTS), F32)),
        in_specs=whole(4),
        out_specs=tuple(whole(2)),
        compiler_params=params(),
        cost_estimate=cost(1 << 29),
        name="place_q",
    )(picked_row, gate_row, dq_own, dq_peer)
    logit_out = pl.pallas_call(
        place_logit_kernel,
        out_shape=shape((TOKENS // SLOTS, SLOTS)),
        in_specs=whole(6),
        out_specs=whole(1)[0],
        compiler_params=params(),
        cost_estimate=cost(1 << 28),
        name="place_logit",
    )(picked_row, closed, *delta_parts)
    k_out, v_out = pl.pallas_call(
        place_kv_kernel,
        out_shape=(shape((TOKENS, HEAD)), shape((TOKENS, HEAD))),
        in_specs=whole(2),
        out_specs=tuple(whole(2)),
        compiler_params=params(),
        name="place_kv",
    )(picked_row, dkv_all)
    return q_out, k_out, v_out, logit_out.reshape(TOKENS)


def solution(mesh):
    split = Mesh(mesh.devices.reshape(4, 4, 2, 8), ("y", "x", "c", "tp"))
    seq = ("y", "x", "c")
    return jax.shard_map(
        local,
        mesh=split,
        in_specs=(P(seq, "tp"), P(seq, "tp"), P(seq, "tp"), P(seq), P(seq, "tp"), P(seq)),
        out_specs=(P(seq, "tp"), P(seq, "tp"), P(seq, "tp"), P(seq)),
        check_vma=False,
    )
```

```python
import functools
import math

import jax
import jax.numpy as jnp
from jax import lax
from jax.experimental import pallas as pl
from jax.experimental.pallas import tpu as pltpu
from jax.sharding import Mesh, PartitionSpec as P

QUERY_HEADS = 64
KEY_VALUE_HEADS = 8
HEAD = 128
SLOTS = 128
TOKENS = 512
CHIPS = 16
PICKED = 2048
GROUP = QUERY_HEADS // KEY_VALUE_HEADS
FACTOR = 1.0 / math.sqrt(HEAD)
LOG_FACTOR = FACTOR * math.log2(math.e)
CHUNK = 32
CHUNKS = SLOTS // CHUNK
ROWS = GROUP * CHUNK
KEYS = 512
EDGE = 256
PART = 128
SPARE = 2 * CHUNKS
KEPT = 1536
KERNEL_BYTES = 16 * 1024 * 1024
SENTINEL = 128.0
LIVE_BELOW = 32.0
NEGATIVE = -1e30
F32 = jnp.float32
BF16 = jnp.bfloat16
VMEM_BYTES = 48 * 1024 * 1024
VMEM_ALL = 64 * 1024 * 1024


def nt_dot(a, b):
    return lax.dot_general(a, b, (((1,), (1,)), ((), ())), preferred_element_type=F32)


def tn_dot(a, b):
    return lax.dot_general(a, b, (((0,), (0,)), ((), ())), preferred_element_type=F32)


def place_matrix(picked):
    token = lax.broadcasted_iota(jnp.int32, (TOKENS, SLOTS), 0)
    return jnp.where(token == picked, 1.0, 0.0).astype(F32)


def switch_of(gate, gather):
    rows = jnp.dot(
        jnp.broadcast_to(gate, (16, TOKENS)), gather.astype(BF16), preferred_element_type=F32
    )
    return 1.0 / (1.0 + jnp.exp(-rows))


def fetch(pairs, sems):
    copies = [pltpu.make_async_copy(src, dst, sems.at[n]) for n, (src, dst) in enumerate(pairs)]
    for copy in copies:
        copy.start()
    for copy in copies:
        copy.wait()


def pick_kv_kernel(picked_hbm, k_hbm, v_hbm, kv_out, picked_ref, k_ref, v_ref, message, sems, out_sems):
    pairs = [(picked_hbm, picked_ref), (k_hbm, k_ref), (v_hbm, v_ref)]
    copies = [pltpu.make_async_copy(src, dst, sems.at[n]) for n, (src, dst) in enumerate(pairs)]
    for copy in copies:
        copy.start()
    copies[0].wait()
    column = jnp.broadcast_to(picked_ref[...], (SLOTS, SLOTS)).astype(F32).T
    token = lax.broadcasted_iota(jnp.int32, (SLOTS, SLOTS), 1).astype(F32)
    gather = jnp.concatenate(
        [jnp.where(token + base == column, 1.0, 0.0) for base in range(0, TOKENS, SLOTS)], axis=1
    ).astype(BF16)
    dead = jnp.where(column >= TOKENS, SENTINEL, 0.0)
    copies[1].wait()
    keys = jnp.dot(gather, k_ref[...], preferred_element_type=F32)
    message[:, 0:HEAD] = (keys + dead).astype(BF16)
    copies[2].wait()
    message[:, HEAD : 2 * HEAD] = jnp.dot(
        gather, v_ref[...], preferred_element_type=F32
    ).astype(BF16)
    fetch([(message, kv_out.at[chip]) for chip in range(CHIPS)], out_sems)


def pick_q_kernel(picked_hbm, gate_ref, q_hbm, up_hbm, qs_out, picked_ref, q_ref, up_ref, sems):
    fetch([(picked_hbm, picked_ref), (q_hbm, q_ref), (up_hbm, up_ref)], sems)
    placed = place_matrix(picked_ref[...])
    gather = placed.T.astype(BF16)
    switch = jnp.broadcast_to(switch_of(gate_ref[...], placed)[0:1], (SLOTS, SLOTS)).T
    for h in range(GROUP):
        lanes = slice(h * HEAD, (h + 1) * HEAD)
        q_rows = jnp.dot(gather, q_ref[:, lanes], preferred_element_type=F32).astype(BF16)
        up_rows = jnp.dot(gather, up_ref[:, lanes], preferred_element_type=F32)
        scaled = (up_rows * switch).astype(BF16)
        for t in range(CHUNKS):
            rows = slice(t * CHUNK, (t + 1) * CHUNK)
            qs_out[0, t, h * CHUNK : (h + 1) * CHUNK, :] = q_rows[rows]
            qs_out[1, t, h * CHUNK : (h + 1) * CHUNK, :] = scaled[rows]


def count_live(block):
    live = jnp.where(block.astype(F32) < LIVE_BELOW, 1.0, 0.0)
    return jnp.sum(live, axis=0, keepdims=True)[0, 0].astype(jnp.int32)


class Tiles:
    def __init__(self, core, offset, count, own_chunks, live_chunks):
        self.offset, self.count = offset, count
        self.own_chunks, self.live_chunks = own_chunks, live_chunks
        self.other_limit = offset + jnp.where(core == 0, count, 0)
        self.number = lax.div(live_chunks + 1, 2)

    def place(self, chunk):
        place = jnp.where(chunk < self.own_chunks, chunk, CHUNKS + chunk - self.own_chunks)
        return jnp.where(chunk < self.live_chunks, place, SPARE)

    def peer_place(self, chunk):
        place = self.place(chunk)
        return jnp.where(place == SPARE, SPARE, lax.rem(place + CHUNKS, 2 * CHUNKS))

    def limit(self, chunk):
        slot = lax.rem(lax.broadcasted_iota(jnp.int32, (1, ROWS), 1), CHUNK)
        own = self.offset + chunk * CHUNK + 1
        step = jnp.where(chunk < self.own_chunks, 1, 0)
        return jnp.where(chunk < self.own_chunks, own, self.other_limit) + slot * step

    def bounds(self, chunk):
        own = chunk < self.own_chunks
        first = self.offset + chunk * CHUNK
        last = jnp.minimum(first + CHUNK, self.offset + self.count)
        return jnp.where(own, first + 1, self.other_limit), jnp.where(own, last, self.other_limit)

    def spans(self, tile):
        low_a, high_a = self.bounds(2 * tile)
        low_b, high_b = self.bounds(2 * tile + 1)
        paired = 2 * tile + 1 < self.live_chunks
        low = jnp.where(paired, jnp.minimum(low_a, low_b), low_a)
        high = jnp.where(paired, jnp.maximum(high_a, high_b), high_a)
        full = lax.div(low, KEYS)
        rest = high - full * KEYS
        wide = lax.div(rest + EDGE - 1, KEYS)
        return full, wide, rest > wide * KEYS

    def limits(self, tile):
        return jnp.concatenate([self.limit(2 * tile), self.limit(2 * tile + 1)], axis=1)

    def sweep(self, tile, block, carry):
        full, wide, narrow = self.spans(tile)
        limits = self.limits(tile)

        def run(first, count, keys, limits, carry):
            def steps(kept):
                return lambda b, carry: block(
                    pl.multiple_of(first + b * keys, keys), keys, limits, kept, carry
                )

            inside = jnp.minimum(jnp.maximum(lax.div(KEPT - first, keys), 0), count)
            carry = lax.fori_loop(0, inside, steps(True), carry)
            return lax.fori_loop(inside, count, steps(False), carry)

        carry = run(0, full, KEYS, None, carry)
        carry = run(full * KEYS, wide, KEYS, limits, carry)
        last = (full + wide) * KEYS
        return run(last, jnp.where(narrow, 1, 0), EDGE, limits, carry)


def pair_rows(tile):
    return pl.ds(pl.multiple_of(tile * 2 * ROWS, 2 * ROWS), 2 * ROWS)


def stats_kernel(
    peer_picked, kv_ref, own_ref, oth_ref, kc_out, vc_out, q_out, s_out, stats_out, raised_out,
    pushed_out, tops_out, info_out, k_pack, v_pack,
):
    chip = lax.axis_index("y") * 4 + lax.axis_index("x")
    core = lax.axis_index("c")
    stats_out[...] = jnp.zeros_like(stats_out)
    offset = 0
    own_offset = 0
    own_count = 0
    counts = [count_live(kv_ref[s, :, 0:HEAD]) for s in range(CHIPS)]
    for s in range(CHIPS):
        k_pack[pl.ds(offset, SLOTS), :] = kv_ref[s, :, 0:HEAD].astype(F32)
        v_pack[pl.ds(offset, SLOTS), :] = kv_ref[s, :, HEAD : 2 * HEAD].astype(F32)
        info_out[s] = jnp.asarray(offset, jnp.int32)
        own_offset = jnp.where(chip == s, offset, own_offset)
        own_count = jnp.where(chip == s, counts[s], own_count)
        offset = offset + counts[s]
    peer_live = jnp.where(peer_picked[...] < TOKENS, 1.0, 0.0)
    other_count = jnp.sum(peer_live, axis=1, keepdims=True)[0, 0].astype(jnp.int32)
    own_chunks = lax.div(own_count + CHUNK - 1, CHUNK)
    live_chunks = own_chunks + lax.div(other_count + CHUNK - 1, CHUNK)
    info_out[16] = own_offset
    info_out[17] = own_count
    info_out[18] = own_chunks
    info_out[19] = live_chunks
    tail = pl.ds(offset + SLOTS, KEYS)
    k_pack[tail, :] = jnp.zeros((KEYS, HEAD), F32)
    v_pack[tail, :] = jnp.zeros((KEYS, HEAD), F32)

    def narrow_keys(b, _):
        rows = pl.ds(pl.multiple_of(b * KEYS, KEYS), KEYS)
        kc_out[rows, :] = k_pack[rows, :].astype(BF16)
        vc_out[rows, :] = v_pack[rows, :].astype(BF16)
        return 0

    lax.fori_loop(0, lax.div(own_offset + own_count + KEYS - 1, KEYS), narrow_keys, 0)
    for t in range(CHUNKS):
        q_out[t * ROWS : (t + 1) * ROWS, :] = own_ref[0, t]
        s_out[t * ROWS : (t + 1) * ROWS, :] = own_ref[1, t]
    for t in range(CHUNKS):
        rows = pl.ds(pl.multiple_of((own_chunks + t) * ROWS, ROWS), ROWS)
        q_out[rows, :] = oth_ref[0, t]
        s_out[rows, :] = oth_ref[1, t]
    spare = pl.ds(pl.multiple_of(live_chunks * ROWS, ROWS), ROWS)
    q_out[spare, :] = jnp.zeros((ROWS, HEAD), BF16)
    s_out[spare, :] = jnp.zeros((ROWS, HEAD), BF16)
    tiles = Tiles(core, own_offset, own_count, own_chunks, live_chunks)

    def attend(tile, _):
        q_rows = q_out[pair_rows(tile), :]
        s_rows = s_out[pair_rows(tile), :]

        def block(base, keys, limits, kept, carry):
            top, total, pull = carry
            scores = nt_dot(kc_out[pl.ds(base, keys), :], q_rows)
            pushed = nt_dot(vc_out[pl.ds(base, keys), :], s_rows)
            if kept:
                pushed_out[tile, pl.ds(base, keys), :] = pushed
            for u in range(0, keys, PART):
                part = scores[u : u + PART] * LOG_FACTOR
                if limits is not None:
                    index = lax.broadcasted_iota(jnp.int32, (PART, 2 * ROWS), 0)
                    part = jnp.where(index < limits - (base + u), part, NEGATIVE)
                part = part.reshape(PART // 8, 8, 2 * ROWS)
                new_top = jnp.maximum(top, jnp.max(part, axis=0))
                raised = jnp.exp2(part - new_top[None])
                if kept:
                    rows = pl.ds(pl.multiple_of(base + u, PART), PART)
                    raised_out[tile, rows, :] = raised.reshape(PART, 2 * ROWS)
                    tops_out[tile, lax.div(base + u, PART)] = new_top
                fade = jnp.exp2(top - new_top)
                total = total * fade + jnp.sum(raised, axis=0)
                pulled = raised * pushed[u : u + PART].reshape(PART // 8, 8, 2 * ROWS)
                pull = pull * fade + jnp.sum(pulled, axis=0)
                top = new_top
            return top, total, pull

        zero = jnp.zeros((8, 2 * ROWS), F32)
        top, total, pull = tiles.sweep(
            tile, block, (jnp.full((8, 2 * ROWS), NEGATIVE, F32), zero, zero)
        )
        best = jnp.max(top, axis=0, keepdims=True)
        fade = jnp.exp2(top - best)
        total = jnp.sum(total * fade, axis=0, keepdims=True)
        pull = jnp.sum(pull * fade, axis=0, keepdims=True)
        for half in range(2):
            place = tiles.place(2 * tile + half)
            lanes = slice(half * ROWS, (half + 1) * ROWS)
            stats_out[place, 0:1, :] = best[:, lanes]
            stats_out[place, 1:2, :] = total[:, lanes]
            stats_out[place, 2:3, :] = pull[:, lanes]
        return 0

    lax.fori_loop(0, tiles.number, attend, 0)


def grad_kernel(
    info_ref, kc_ref, vc_ref, q_ref, s_ref, stats_ref, peer_ref, raised_ref, pushed_ref, tops_ref, dkv_out, dq_own, dq_oth, delta_out,
    dk_sum, dv_sum, dq_sum, message, sems,
):
    core = lax.axis_index("c")
    tiles = Tiles(core, info_ref[16], info_ref[17], info_ref[18], info_ref[19])
    dk_sum[...] = jnp.zeros_like(dk_sum)
    dv_sum[...] = jnp.zeros_like(dv_sum)
    dq_own[...] = jnp.zeros_like(dq_own)
    dq_oth[...] = jnp.zeros_like(dq_oth)
    delta_out[...] = jnp.zeros_like(delta_out)

    def push_back(tile, _):
        q_rows = q_ref[pair_rows(tile), :]
        s_rows = s_ref[pair_rows(tile), :]
        chunks = (2 * tile, 2 * tile + 1)
        mine = jnp.concatenate([stats_ref[tiles.place(c)] for c in chunks], axis=1)
        theirs = jnp.concatenate([peer_ref[tiles.peer_place(c)] for c in chunks], axis=1)
        top = jnp.maximum(mine[0:1], theirs[0:1])
        mine_scale = jnp.exp2(mine[0:1] - top)
        their_scale = jnp.exp2(theirs[0:1] - top)
        total = mine[1:2] * mine_scale + theirs[1:2] * their_scale
        total = jnp.where(total > 0.0, total, 1.0)
        delta = (mine[2:3] * mine_scale + theirs[2:3] * their_scale) / total
        level = top + jnp.log2(total)
        lane = lax.div(lax.broadcasted_iota(jnp.int32, (1, SLOTS), 1), CHUNK)
        for half, chunk in enumerate(chunks):
            first = half * ROWS
            heads = delta[:, first : first + 128] + delta[:, first + 128 : first + 256]
            heads = heads + pltpu.roll(heads, 64, 1)
            heads = heads + pltpu.roll(heads, 32, 1)
            mark = jnp.where(chunk < tiles.own_chunks, chunk, CHUNKS)
            delta_out[0:1, :] += jnp.where(lane == mark, heads, 0.0)
        dq_sum[...] = jnp.zeros_like(dq_sum)

        def block(base, keys, limits, kept, carry):
            span = pl.ds(base, keys)
            key_rows = kc_ref[span, :]
            if kept:
                pushed = pushed_ref[tile, span, :]
                parts = []
                for u in range(0, keys, PART):
                    rows = pl.ds(pl.multiple_of(base + u, PART), PART)
                    scale = jnp.exp2(tops_ref[tile, lax.div(base + u, PART)] - level)
                    part = raised_ref[tile, rows, :].reshape(PART // 8, 8, 2 * ROWS)
                    parts.append((part * scale[None]).reshape(PART, 2 * ROWS))
                weights = jnp.concatenate(parts, axis=0)
            else:
                scores = nt_dot(key_rows, q_rows)
                pushed = nt_dot(vc_ref[span, :], s_rows)
                weights = jnp.exp2(scores * LOG_FACTOR - level)
                if limits is not None:
                    index = lax.broadcasted_iota(jnp.int32, (keys, 2 * ROWS), 0)
                    weights = jnp.where(index < limits - base, weights, 0.0)
            slopes = (weights * (pushed - delta)).astype(BF16)
            dv_sum[span, :] += jnp.dot(
                weights.astype(BF16), s_rows, preferred_element_type=F32
            )
            dk_sum[span, :] += jnp.dot(slopes, q_rows, preferred_element_type=F32)
            dq_sum[...] += tn_dot(slopes, key_rows)
            return carry

        tiles.sweep(tile, block, 0)
        for half, chunk in enumerate(chunks):
            rows = slice(half * ROWS, (half + 1) * ROWS)

            @pl.when(chunk < tiles.own_chunks)
            def _():
                dq_own[chunk] = dq_sum[rows, :]

            @pl.when((chunk >= tiles.own_chunks) & (chunk < tiles.live_chunks))
            def _():
                dq_oth[chunk - tiles.own_chunks] = dq_sum[rows, :].astype(BF16)

        return 0

    lax.fori_loop(0, tiles.number, push_back, 0)
    copies = []
    for s in range(CHIPS):
        rows = pl.ds(info_ref[s], SLOTS)
        message[s, :, 0:HEAD] = dk_sum[rows, :].astype(BF16)
        message[s, :, HEAD : 2 * HEAD] = dv_sum[rows, :].astype(BF16)
        copies.append(pltpu.make_async_copy(message.at[s], dkv_out.at[(s % 4) * 4 + s // 4], sems.at[s]))
        copies[s].start()
    for copy in copies:
        copy.wait()


def place_q_kernel(picked_ref, gate_ref, dq_own, dq_peer, q_out, closed_out):
    placed = place_matrix(picked_ref[...])
    scatter = placed.astype(BF16)
    closed_out[...] = 1.0 - switch_of(gate_ref[...], placed)[0:8]
    for h in range(GROUP):
        rows = slice(h * CHUNK, (h + 1) * CHUNK)
        parts = [
            ((dq_own[t, rows, :] + dq_peer[t, rows, :].astype(F32)) * FACTOR).astype(BF16)
            for t in range(CHUNKS)
        ]
        q_out[:, h * HEAD : (h + 1) * HEAD] = jnp.dot(
            scatter, jnp.concatenate(parts, axis=0), preferred_element_type=F32
        ).astype(BF16)


def place_kv_kernel(
    picked_ref, dkv_ref, part_a, part_b, part_c, part_d, k_out, v_out, logit_out
):
    scatter = place_matrix(picked_ref[...]).astype(BF16)
    total = dkv_ref[0].astype(F32)
    for s in range(1, CHIPS):
        total = total + dkv_ref[s].astype(F32)
    k_rows = (total[:, 0:HEAD] * FACTOR).astype(BF16)
    v_rows = total[:, HEAD : 2 * HEAD].astype(BF16)
    k_out[...] = jnp.dot(scatter, k_rows, preferred_element_type=F32).astype(BF16)
    v_out[...] = jnp.dot(scatter, v_rows, preferred_element_type=F32).astype(BF16)
    logits = (part_a[...] + part_b[...]) + (part_c[...] + part_d[...])
    logit_rows = jnp.concatenate([logits, logits], axis=0).astype(BF16)
    for part in range(TOKENS // SLOTS):
        rows = slice(part * SLOTS, (part + 1) * SLOTS)
        logit_out[part : part + 1, :] = nt_dot(logit_rows, scatter[rows])[0:1].astype(BF16)


def whole(count):
    return [pl.BlockSpec(memory_space=pltpu.VMEM)] * count


def params(limit=VMEM_BYTES):
    return pltpu.CompilerParams(vmem_limit_bytes=limit)


def shape(dims, kind=BF16):
    return jax.ShapeDtypeStruct(dims, kind)


def hbm(count):
    return [pl.BlockSpec(memory_space=pltpu.HBM)] * count


def cost(flops):
    return pl.CostEstimate(flops=flops, bytes_accessed=1 << 20, transcendentals=0)


def local(head_queries, key_projection_rows, value_projection_rows, gate_logit, upstream, picked):
    picked_row = picked.reshape(1, SLOTS)
    swap = [(0, 1), (1, 0)]
    kv_copies = pl.pallas_call(
        pick_kv_kernel,
        out_shape=shape((CHIPS, SLOTS, 2 * HEAD)),
        in_specs=hbm(3),
        out_specs=hbm(1)[0],
        scratch_shapes=[
            pltpu.VMEM((1, SLOTS), jnp.int32),
            pltpu.VMEM((TOKENS, HEAD), BF16),
            pltpu.VMEM((TOKENS, HEAD), BF16),
            pltpu.VMEM((SLOTS, 2 * HEAD), BF16),
            pltpu.SemaphoreType.DMA((3,)),
            pltpu.SemaphoreType.DMA((CHIPS,)),
        ],
        compiler_params=params(VMEM_ALL),
        name="pick_kv",
    )(picked_row, key_projection_rows, value_projection_rows)
    kv_all = lax.all_to_all(kv_copies, ("y", "x"), 0, 0, tiled=True)
    gate_row = gate_logit.reshape(1, TOKENS)
    qs_own = pl.pallas_call(
        pick_q_kernel,
        out_shape=shape((2, CHUNKS, ROWS, HEAD)),
        in_specs=hbm(1) + whole(1) + hbm(2),
        out_specs=whole(1)[0],
        scratch_shapes=[
            pltpu.VMEM((1, SLOTS), jnp.int32),
            pltpu.VMEM((TOKENS, GROUP * HEAD), BF16),
            pltpu.VMEM((TOKENS, GROUP * HEAD), BF16),
            pltpu.SemaphoreType.DMA((3,)),
        ],
        compiler_params=params(),
        cost_estimate=cost(1 << 30),
        name="pick_q",
    )(picked_row, gate_row, head_queries, upstream)
    qs_peer = lax.ppermute(qs_own, "c", swap)
    peer_picked = lax.ppermute(picked_row, "c", swap)
    kc, vc, q_rows, s_rows, stats, raised, pushed, tops, info = pl.pallas_call(
        stats_kernel,
        out_shape=(
            shape((PICKED, HEAD)),
            shape((PICKED, HEAD)),
            shape(((2 * CHUNKS + 1) * ROWS, HEAD)),
            shape(((2 * CHUNKS + 1) * ROWS, HEAD)),
            shape((SPARE + 1, 8, ROWS), F32),
            shape((CHUNKS, KEPT, 2 * ROWS), F32),
            shape((CHUNKS, KEPT, 2 * ROWS), F32),
            shape((CHUNKS, KEPT // PART, 8, 2 * ROWS), F32),
            shape((32,), jnp.int32),
        ),
        in_specs=whole(4),
        out_specs=tuple(whole(8)) + (pl.BlockSpec(memory_space=pltpu.SMEM),),
        scratch_shapes=[pltpu.VMEM((PICKED + SLOTS + KEYS, HEAD), F32)] * 2,
        compiler_params=params(KERNEL_BYTES),
        name="stats",
    )(peer_picked, kv_all, qs_own, qs_peer)
    stats_peer = lax.ppermute(stats, "c", swap)
    dkv, dq_own, dq_oth, deltas = pl.pallas_call(
        grad_kernel,
        out_shape=(
            shape((CHIPS, SLOTS, 2 * HEAD)),
            shape((CHUNKS, ROWS, HEAD), F32),
            shape((CHUNKS, ROWS, HEAD)),
            shape((8, SLOTS), F32),
        ),
        in_specs=[pl.BlockSpec(memory_space=pltpu.SMEM)] + whole(9),
        out_specs=tuple(hbm(1) + whole(3)),
        scratch_shapes=[
            pltpu.VMEM((PICKED + SLOTS, HEAD), F32),
            pltpu.VMEM((PICKED + SLOTS, HEAD), F32),
            pltpu.VMEM((2 * ROWS, HEAD), F32),
            pltpu.VMEM((CHIPS, SLOTS, 2 * HEAD), BF16),
            pltpu.SemaphoreType.DMA((CHIPS,)),
        ],
        compiler_params=params(KERNEL_BYTES),
        cost_estimate=cost(1 << 32),
        name="grads",
    )(info, kc, vc, q_rows, s_rows, stats, stats_peer, raised, pushed, tops)
    dkv_all = lax.all_to_all(dkv, ("x", "y"), 0, 0, tiled=True)
    delta_far = lax.ppermute(deltas, "tp", [(i, i ^ 4) for i in range(8)])
    dq_peer = lax.ppermute(dq_oth, "c", swap)
    q_out, closed = pl.pallas_call(
        place_q_kernel,
        out_shape=(shape((TOKENS, GROUP * HEAD)), shape((8, SLOTS), F32)),
        in_specs=whole(4),
        out_specs=tuple(whole(2)),
        compiler_params=params(),
        cost_estimate=cost(1 << 29),
        name="place_q",
    )(picked_row, gate_row, dq_own, dq_peer)
    logit_half = (deltas + delta_far) * closed
    logit_parts = [logit_half] + [
        lax.ppermute(logit_half, "tp", [(i, i ^ k) for i in range(8)]) for k in (1, 2, 3)
    ]
    k_out, v_out, logit_out = pl.pallas_call(
        place_kv_kernel,
        out_shape=(
            shape((TOKENS, HEAD)),
            shape((TOKENS, HEAD)),
            shape((TOKENS // SLOTS, SLOTS)),
        ),
        in_specs=whole(6),
        out_specs=tuple(whole(3)),
        compiler_params=params(),
        name="place_kv",
    )(picked_row, dkv_all, *logit_parts)
    return q_out, k_out, v_out, logit_out.reshape(TOKENS)


def solution(mesh):
    split = Mesh(mesh.devices.reshape(4, 4, 2, 8), ("y", "x", "c", "tp"))
    seq = ("y", "x", "c")
    return jax.shard_map(
        local,
        mesh=split,
        in_specs=(P(seq, "tp"), P(seq, "tp"), P(seq, "tp"), P(seq), P(seq, "tp"), P(seq)),
        out_specs=(P(seq, "tp"), P(seq, "tp"), P(seq, "tp"), P(seq)),
        check_vma=False,
    )
```

```python
import functools
import math

import jax
import jax.numpy as jnp
from jax import lax
from jax.experimental import pallas as pl
from jax.experimental.pallas import tpu as pltpu
from jax.sharding import Mesh, PartitionSpec as P

QUERY_HEADS = 64
KEY_VALUE_HEADS = 8
HEAD = 128
SLOTS = 128
TOKENS = 512
CHIPS = 16
PICKED = 2048
GROUP = QUERY_HEADS // KEY_VALUE_HEADS
FACTOR = 1.0 / math.sqrt(HEAD)
LOG_FACTOR = FACTOR * math.log2(math.e)
CHUNK = 32
CHUNKS = SLOTS // CHUNK
ROWS = GROUP * CHUNK
KEYS = 512
EDGE = 256
PART = 128
SPARE = 2 * CHUNKS
KEPT = 1536
KERNEL_BYTES = 16 * 1024 * 1024
SENTINEL = 128.0
LIVE_BELOW = 32.0
NEGATIVE = -1e30
F32 = jnp.float32
BF16 = jnp.bfloat16
VMEM_BYTES = 48 * 1024 * 1024
VMEM_ALL = 64 * 1024 * 1024


def nt_dot(a, b):
    return lax.dot_general(a, b, (((1,), (1,)), ((), ())), preferred_element_type=F32)


def tn_dot(a, b):
    return lax.dot_general(a, b, (((0,), (0,)), ((), ())), preferred_element_type=F32)


def place_matrix(picked):
    token = lax.broadcasted_iota(jnp.int32, (TOKENS, SLOTS), 0)
    return jnp.where(token == picked, 1.0, 0.0).astype(F32)


def switch_of(gate, gather):
    rows = jnp.dot(
        jnp.broadcast_to(gate, (16, TOKENS)), gather.astype(BF16), preferred_element_type=F32
    )
    return 1.0 / (1.0 + jnp.exp(-rows))


def fetch(pairs, sems):
    copies = [pltpu.make_async_copy(src, dst, sems.at[n]) for n, (src, dst) in enumerate(pairs)]
    for copy in copies:
        copy.start()
    for copy in copies:
        copy.wait()


def pick_kv_kernel(picked_hbm, k_hbm, v_hbm, kv_out, picked_ref, k_ref, v_ref, message, sems, out_sems):
    pairs = [(picked_hbm, picked_ref), (k_hbm, k_ref), (v_hbm, v_ref)]
    copies = [pltpu.make_async_copy(src, dst, sems.at[n]) for n, (src, dst) in enumerate(pairs)]
    for copy in copies:
        copy.start()
    copies[0].wait()
    column = jnp.broadcast_to(picked_ref[...], (SLOTS, SLOTS)).astype(F32).T
    token = lax.broadcasted_iota(jnp.int32, (SLOTS, SLOTS), 1).astype(F32)
    gather = jnp.concatenate(
        [jnp.where(token + base == column, 1.0, 0.0) for base in range(0, TOKENS, SLOTS)], axis=1
    ).astype(BF16)
    dead = jnp.where(column >= TOKENS, SENTINEL, 0.0)
    copies[1].wait()
    keys = jnp.dot(gather, k_ref[...], preferred_element_type=F32)
    message[:, 0:HEAD] = (keys + dead).astype(BF16)
    copies[2].wait()
    message[:, HEAD : 2 * HEAD] = jnp.dot(
        gather, v_ref[...], preferred_element_type=F32
    ).astype(BF16)
    fetch([(message, kv_out.at[chip]) for chip in range(CHIPS)], out_sems)


def pick_q_kernel(picked_hbm, gate_ref, q_hbm, up_hbm, qs_out, picked_ref, q_ref, up_ref, sems):
    fetch([(picked_hbm, picked_ref), (q_hbm, q_ref), (up_hbm, up_ref)], sems)
    placed = place_matrix(picked_ref[...])
    gather = placed.T.astype(BF16)
    switch = jnp.broadcast_to(switch_of(gate_ref[...], placed)[0:1], (SLOTS, SLOTS)).T
    for h in range(GROUP):
        lanes = slice(h * HEAD, (h + 1) * HEAD)
        q_rows = jnp.dot(gather, q_ref[:, lanes], preferred_element_type=F32).astype(BF16)
        up_rows = jnp.dot(gather, up_ref[:, lanes], preferred_element_type=F32)
        scaled = (up_rows * switch).astype(BF16)
        for t in range(CHUNKS):
            rows = slice(t * CHUNK, (t + 1) * CHUNK)
            qs_out[0, t, h * CHUNK : (h + 1) * CHUNK, :] = q_rows[rows]
            qs_out[1, t, h * CHUNK : (h + 1) * CHUNK, :] = scaled[rows]


def count_live(block):
    live = jnp.where(block.astype(F32) < LIVE_BELOW, 1.0, 0.0)
    return jnp.sum(live, axis=0, keepdims=True)[0, 0].astype(jnp.int32)


class Tiles:
    def __init__(self, core, offset, count, own_chunks, live_chunks):
        self.offset, self.count = offset, count
        self.own_chunks, self.live_chunks = own_chunks, live_chunks
        self.other_limit = offset + jnp.where(core == 0, count, 0)
        self.number = lax.div(live_chunks + 1, 2)

    def place(self, chunk):
        place = jnp.where(chunk < self.own_chunks, chunk, CHUNKS + chunk - self.own_chunks)
        return jnp.where(chunk < self.live_chunks, place, SPARE)

    def limit(self, chunk):
        slot = lax.rem(lax.broadcasted_iota(jnp.int32, (1, ROWS), 1), CHUNK)
        own = self.offset + chunk * CHUNK + 1
        step = jnp.where(chunk < self.own_chunks, 1, 0)
        return jnp.where(chunk < self.own_chunks, own, self.other_limit) + slot * step

    def bounds(self, chunk):
        own = chunk < self.own_chunks
        first = self.offset + chunk * CHUNK
        last = jnp.minimum(first + CHUNK, self.offset + self.count)
        return jnp.where(own, first + 1, self.other_limit), jnp.where(own, last, self.other_limit)

    def spans(self, tile):
        low_a, high_a = self.bounds(2 * tile)
        low_b, high_b = self.bounds(2 * tile + 1)
        paired = 2 * tile + 1 < self.live_chunks
        low = jnp.where(paired, jnp.minimum(low_a, low_b), low_a)
        high = jnp.where(paired, jnp.maximum(high_a, high_b), high_a)
        full = lax.div(low, KEYS)
        rest = high - full * KEYS
        wide = lax.div(rest + EDGE - 1, KEYS)
        return full, wide, rest > wide * KEYS

    def limits(self, tile):
        return jnp.concatenate([self.limit(2 * tile), self.limit(2 * tile + 1)], axis=1)

    def sweep(self, tile, block, carry):
        full, wide, narrow = self.spans(tile)
        limits = self.limits(tile)

        def run(first, count, keys, limits, carry):
            def steps(kept):
                return lambda b, carry: block(
                    pl.multiple_of(first + b * keys, keys), keys, limits, kept, carry
                )

            inside = jnp.minimum(jnp.maximum(lax.div(KEPT - first, keys), 0), count)
            carry = lax.fori_loop(0, inside, steps(True), carry)
            return lax.fori_loop(inside, count, steps(False), carry)

        carry = run(0, full, KEYS, None, carry)
        carry = run(full * KEYS, wide, KEYS, limits, carry)
        last = (full + wide) * KEYS
        return run(last, jnp.where(narrow, 1, 0), EDGE, limits, carry)


def pair_rows(tile):
    return pl.ds(pl.multiple_of(tile * 2 * ROWS, 2 * ROWS), 2 * ROWS)


def stats_kernel(
    peer_picked, kv_ref, own_ref, oth_ref, kc_out, vc_out, q_out, s_out, stats_out, raised_out,
    pushed_out, tops_out, info_out, k_pack, v_pack,
):
    chip = lax.axis_index("y") * 4 + lax.axis_index("x")
    core = lax.axis_index("c")
    stats_out[...] = jnp.zeros_like(stats_out)
    offset = 0
    own_offset = 0
    own_count = 0
    counts = [count_live(kv_ref[s, :, 0:HEAD]) for s in range(CHIPS)]
    for s in range(CHIPS):
        k_pack[pl.ds(offset, SLOTS), :] = kv_ref[s, :, 0:HEAD].astype(F32)
        v_pack[pl.ds(offset, SLOTS), :] = kv_ref[s, :, HEAD : 2 * HEAD].astype(F32)
        info_out[s] = jnp.asarray(offset, jnp.int32)
        own_offset = jnp.where(chip == s, offset, own_offset)
        own_count = jnp.where(chip == s, counts[s], own_count)
        offset = offset + counts[s]
    peer_live = jnp.where(peer_picked[...] < TOKENS, 1.0, 0.0)
    other_count = jnp.sum(peer_live, axis=1, keepdims=True)[0, 0].astype(jnp.int32)
    own_chunks = lax.div(own_count + CHUNK - 1, CHUNK)
    live_chunks = own_chunks + lax.div(other_count + CHUNK - 1, CHUNK)
    info_out[16] = own_offset
    info_out[17] = own_count
    info_out[18] = own_chunks
    info_out[19] = live_chunks
    tail = pl.ds(offset + SLOTS, KEYS)
    k_pack[tail, :] = jnp.zeros((KEYS, HEAD), F32)
    v_pack[tail, :] = jnp.zeros((KEYS, HEAD), F32)

    def narrow_keys(b, _):
        rows = pl.ds(pl.multiple_of(b * KEYS, KEYS), KEYS)
        kc_out[rows, :] = k_pack[rows, :].astype(BF16)
        vc_out[rows, :] = v_pack[rows, :].astype(BF16)
        return 0

    lax.fori_loop(0, lax.div(own_offset + own_count + KEYS - 1, KEYS), narrow_keys, 0)
    for t in range(CHUNKS):
        q_out[t * ROWS : (t + 1) * ROWS, :] = own_ref[0, t]
        s_out[t * ROWS : (t + 1) * ROWS, :] = own_ref[1, t]
    for t in range(CHUNKS):
        rows = pl.ds(pl.multiple_of((own_chunks + t) * ROWS, ROWS), ROWS)
        q_out[rows, :] = oth_ref[0, t]
        s_out[rows, :] = oth_ref[1, t]
    spare = pl.ds(pl.multiple_of(live_chunks * ROWS, ROWS), ROWS)
    q_out[spare, :] = jnp.zeros((ROWS, HEAD), BF16)
    s_out[spare, :] = jnp.zeros((ROWS, HEAD), BF16)
    tiles = Tiles(core, own_offset, own_count, own_chunks, live_chunks)

    def attend(tile, _):
        q_rows = q_out[pair_rows(tile), :]
        s_rows = s_out[pair_rows(tile), :]

        def block(base, keys, limits, kept, carry):
            top, total, pull = carry
            scores = nt_dot(kc_out[pl.ds(base, keys), :], q_rows)
            pushed = nt_dot(vc_out[pl.ds(base, keys), :], s_rows)
            if kept:
                pushed_out[tile, pl.ds(base, keys), :] = pushed
            for u in range(0, keys, PART):
                part = scores[u : u + PART] * LOG_FACTOR
                if limits is not None:
                    index = lax.broadcasted_iota(jnp.int32, (PART, 2 * ROWS), 0)
                    part = jnp.where(index < limits - (base + u), part, NEGATIVE)
                part = part.reshape(PART // 8, 8, 2 * ROWS)
                new_top = jnp.maximum(top, jnp.max(part, axis=0))
                raised = jnp.exp2(part - new_top[None])
                if kept:
                    rows = pl.ds(pl.multiple_of(base + u, PART), PART)
                    raised_out[tile, rows, :] = raised.reshape(PART, 2 * ROWS)
                    tops_out[tile, lax.div(base + u, PART)] = new_top
                fade = jnp.exp2(top - new_top)
                total = total * fade + jnp.sum(raised, axis=0)
                pulled = raised * pushed[u : u + PART].reshape(PART // 8, 8, 2 * ROWS)
                pull = pull * fade + jnp.sum(pulled, axis=0)
                top = new_top
            return top, total, pull

        zero = jnp.zeros((8, 2 * ROWS), F32)
        top, total, pull = tiles.sweep(
            tile, block, (jnp.full((8, 2 * ROWS), NEGATIVE, F32), zero, zero)
        )
        best = jnp.max(top, axis=0, keepdims=True)
        fade = jnp.exp2(top - best)
        total = jnp.sum(total * fade, axis=0, keepdims=True)
        pull = jnp.sum(pull * fade, axis=0, keepdims=True)
        for half in range(2):
            place = tiles.place(2 * tile + half)
            lanes = slice(half * ROWS, (half + 1) * ROWS)
            stats_out[place, 0:1, :] = best[:, lanes]
            stats_out[place, 1:2, :] = total[:, lanes]
            stats_out[place, 2:3, :] = pull[:, lanes]
        return 0

    lax.fori_loop(0, tiles.number, attend, 0)


def combine_kernel(info_ref, stats_ref, peer_ref, comb_out, delta_out):
    own_chunks = info_ref[18]
    lane = lax.div(lax.broadcasted_iota(jnp.int32, (1, SLOTS), 1), CHUNK)
    comb_out[SPARE] = jnp.zeros((8, ROWS), F32)
    deltas = jnp.zeros((1, SLOTS), F32)
    for place in range(SPARE):
        mine = stats_ref[place]
        theirs = peer_ref[(place + CHUNKS) % SPARE]
        top = jnp.maximum(mine[0:1], theirs[0:1])
        mine_scale = jnp.exp2(mine[0:1] - top)
        their_scale = jnp.exp2(theirs[0:1] - top)
        total = mine[1:2] * mine_scale + theirs[1:2] * their_scale
        total = jnp.where(total > 0.0, total, 1.0)
        delta = (mine[2:3] * mine_scale + theirs[2:3] * their_scale) / total
        comb_out[place, 0:1, :] = top + jnp.log2(total)
        comb_out[place, 1:2, :] = delta
        if place < CHUNKS:
            heads = delta[:, 0:128] + delta[:, 128:256]
            heads = heads + pltpu.roll(heads, 64, 1)
            heads = heads + pltpu.roll(heads, 32, 1)
            mark = jnp.where(place < own_chunks, place, CHUNKS)
            deltas = deltas + jnp.where(lane == mark, heads, 0.0)
    delta_out[...] = jnp.broadcast_to(deltas, (8, SLOTS))


def grad_kernel(
    info_ref, kc_ref, vc_ref, q_ref, s_ref, comb_ref, raised_ref, pushed_ref, tops_ref,
    line_0, line_1, line_2, line_3, dq_own, dq_oth, dk_sum, dv_sum, dq_sum,
):
    core = lax.axis_index("c")
    tiles = Tiles(core, info_ref[16], info_ref[17], info_ref[18], info_ref[19])
    dk_sum[...] = jnp.zeros_like(dk_sum)
    dv_sum[...] = jnp.zeros_like(dv_sum)
    dq_own[...] = jnp.zeros_like(dq_own)
    dq_oth[...] = jnp.zeros_like(dq_oth)

    def push_back(tile, _):
        q_rows = q_ref[pair_rows(tile), :]
        s_rows = s_ref[pair_rows(tile), :]
        chunks = (2 * tile, 2 * tile + 1)
        comb = jnp.concatenate([comb_ref[tiles.place(c)] for c in chunks], axis=1)
        level, delta = comb[0:1], comb[1:2]
        dq_sum[...] = jnp.zeros_like(dq_sum)

        def block(base, keys, limits, kept, carry):
            span = pl.ds(base, keys)
            key_rows = kc_ref[span, :]
            if kept:
                pushed = pushed_ref[tile, span, :]
                parts = []
                for u in range(0, keys, PART):
                    rows = pl.ds(pl.multiple_of(base + u, PART), PART)
                    scale = jnp.exp2(tops_ref[tile, lax.div(base + u, PART)] - level)
                    part = raised_ref[tile, rows, :].reshape(PART // 8, 8, 2 * ROWS)
                    parts.append((part * scale[None]).reshape(PART, 2 * ROWS))
                weights = jnp.concatenate(parts, axis=0)
            else:
                scores = nt_dot(key_rows, q_rows)
                pushed = nt_dot(vc_ref[span, :], s_rows)
                weights = jnp.exp2(scores * LOG_FACTOR - level)
                if limits is not None:
                    index = lax.broadcasted_iota(jnp.int32, (keys, 2 * ROWS), 0)
                    weights = jnp.where(index < limits - base, weights, 0.0)
            slopes = (weights * (pushed - delta)).astype(BF16)
            dv_sum[span, :] += jnp.dot(
                weights.astype(BF16), s_rows, preferred_element_type=F32
            )
            dk_sum[span, :] += jnp.dot(slopes, q_rows, preferred_element_type=F32)
            dq_sum[...] += tn_dot(slopes, key_rows)
            return carry

        tiles.sweep(tile, block, 0)
        for half, chunk in enumerate(chunks):
            rows = slice(half * ROWS, (half + 1) * ROWS)

            @pl.when(chunk < tiles.own_chunks)
            def _():
                dq_own[chunk] = dq_sum[rows, :]

            @pl.when((chunk >= tiles.own_chunks) & (chunk < tiles.live_chunks))
            def _():
                dq_oth[chunk - tiles.own_chunks] = dq_sum[rows, :].astype(BF16)

        return 0

    lax.fori_loop(0, tiles.number, push_back, 0)
    row, column = lax.axis_index("y"), lax.axis_index("x")
    for k, line in enumerate((line_0, line_1, line_2, line_3)):
        for j in range(4):
            down, right = jnp.where(core == 0, k, j), jnp.where(core == 0, j, k)
            chip = lax.rem(row + down, 4) * 4 + lax.rem(column + right, 4)
            rows = pl.ds(info_ref[chip], SLOTS)
            line[j, :, 0:HEAD] = dk_sum[rows, :].astype(BF16)
            line[j, :, HEAD : 2 * HEAD] = dv_sum[rows, :].astype(BF16)


def place_q_kernel(picked_ref, gate_ref, dq_own, dq_peer, q_out, closed_out):
    placed = place_matrix(picked_ref[...])
    scatter = placed.astype(BF16)
    closed_out[...] = 1.0 - switch_of(gate_ref[...], placed)[0:8]
    for h in range(GROUP):
        rows = slice(h * CHUNK, (h + 1) * CHUNK)
        parts = [
            ((dq_own[t, rows, :] + dq_peer[t, rows, :].astype(F32)) * FACTOR).astype(BF16)
            for t in range(CHUNKS)
        ]
        q_out[:, h * HEAD : (h + 1) * HEAD] = jnp.dot(
            scatter, jnp.concatenate(parts, axis=0), preferred_element_type=F32
        ).astype(BF16)


def place_kv_kernel(
    picked_ref, closed_ref, own_ref, sum_1, sum_2, sum_3, part_a, part_b, k_out, v_out, logit_out
):
    scatter = place_matrix(picked_ref[...]).astype(BF16)
    total = own_ref[...]
    for other in (sum_1, sum_2, sum_3):
        total = total + other[...].astype(F32)
    k_rows = (total[:, 0:HEAD] * FACTOR).astype(BF16)
    v_rows = total[:, HEAD : 2 * HEAD].astype(BF16)
    k_out[...] = jnp.dot(scatter, k_rows, preferred_element_type=F32).astype(BF16)
    v_out[...] = jnp.dot(scatter, v_rows, preferred_element_type=F32).astype(BF16)
    logits = (part_a[...] + part_b[...]) * closed_ref[...]
    logit_rows = jnp.concatenate([logits, logits], axis=0).astype(BF16)
    for part in range(TOKENS // SLOTS):
        rows = slice(part * SLOTS, (part + 1) * SLOTS)
        logit_out[part : part + 1, :] = nt_dot(logit_rows, scatter[rows])[0:1].astype(BF16)


def whole(count):
    return [pl.BlockSpec(memory_space=pltpu.VMEM)] * count


def params(limit=VMEM_BYTES):
    return pltpu.CompilerParams(vmem_limit_bytes=limit)


def shape(dims, kind=BF16):
    return jax.ShapeDtypeStruct(dims, kind)


def hbm(count):
    return [pl.BlockSpec(memory_space=pltpu.HBM)] * count


def cost(flops):
    return pl.CostEstimate(flops=flops, bytes_accessed=1 << 20, transcendentals=0)


def across(block, step, first):
    def device(y, x, c):
        return (y % 4 * 4 + x % 4) * 2 + c

    pairs = []
    for y in range(4):
        for x in range(4):
            for c in range(2):
                along_x = (c == 0) == first
                target = device(y, x + step, c) if along_x else device(y + step, x, c)
                pairs.append((device(y, x, c), target))
    return lax.ppermute(block, ("y", "x", "c"), pairs)


def local(head_queries, key_projection_rows, value_projection_rows, gate_logit, upstream, picked):
    picked_row = picked.reshape(1, SLOTS)
    swap = [(0, 1), (1, 0)]
    kv_copies = pl.pallas_call(
        pick_kv_kernel,
        out_shape=shape((CHIPS, SLOTS, 2 * HEAD)),
        in_specs=hbm(3),
        out_specs=hbm(1)[0],
        scratch_shapes=[
            pltpu.VMEM((1, SLOTS), jnp.int32),
            pltpu.VMEM((TOKENS, HEAD), BF16),
            pltpu.VMEM((TOKENS, HEAD), BF16),
            pltpu.VMEM((SLOTS, 2 * HEAD), BF16),
            pltpu.SemaphoreType.DMA((3,)),
            pltpu.SemaphoreType.DMA((CHIPS,)),
        ],
        compiler_params=params(VMEM_ALL),
        name="pick_kv",
    )(picked_row, key_projection_rows, value_projection_rows)
    kv_all = lax.all_to_all(kv_copies, ("y", "x"), 0, 0, tiled=True)
    gate_row = gate_logit.reshape(1, TOKENS)
    qs_own = pl.pallas_call(
        pick_q_kernel,
        out_shape=shape((2, CHUNKS, ROWS, HEAD)),
        in_specs=hbm(1) + whole(1) + hbm(2),
        out_specs=whole(1)[0],
        scratch_shapes=[
            pltpu.VMEM((1, SLOTS), jnp.int32),
            pltpu.VMEM((TOKENS, GROUP * HEAD), BF16),
            pltpu.VMEM((TOKENS, GROUP * HEAD), BF16),
            pltpu.SemaphoreType.DMA((3,)),
        ],
        compiler_params=params(),
        cost_estimate=cost(1 << 30),
        name="pick_q",
    )(picked_row, gate_row, head_queries, upstream)
    qs_peer = lax.ppermute(qs_own, "c", swap)
    peer_picked = lax.ppermute(picked_row, "c", swap)
    kc, vc, q_rows, s_rows, stats, raised, pushed, tops, info = pl.pallas_call(
        stats_kernel,
        out_shape=(
            shape((PICKED, HEAD)),
            shape((PICKED, HEAD)),
            shape(((2 * CHUNKS + 1) * ROWS, HEAD)),
            shape(((2 * CHUNKS + 1) * ROWS, HEAD)),
            shape((SPARE + 1, 8, ROWS), F32),
            shape((CHUNKS, KEPT, 2 * ROWS), F32),
            shape((CHUNKS, KEPT, 2 * ROWS), F32),
            shape((CHUNKS, KEPT // PART, 8, 2 * ROWS), F32),
            shape((32,), jnp.int32),
        ),
        in_specs=whole(4),
        out_specs=tuple(whole(8)) + (pl.BlockSpec(memory_space=pltpu.SMEM),),
        scratch_shapes=[pltpu.VMEM((PICKED + SLOTS + KEYS, HEAD), F32)] * 2,
        compiler_params=params(KERNEL_BYTES),
        name="stats",
    )(peer_picked, kv_all, qs_own, qs_peer)
    stats_peer = lax.ppermute(stats, "c", swap)
    comb, deltas = pl.pallas_call(
        combine_kernel,
        out_shape=(shape((SPARE + 1, 8, ROWS), F32), shape((8, SLOTS), F32)),
        in_specs=[pl.BlockSpec(memory_space=pltpu.SMEM)] + whole(2),
        out_specs=tuple(whole(2)),
        compiler_params=params(KERNEL_BYTES),
        name="combine",
    )(info, stats, stats_peer)
    delta_near = lax.ppermute(deltas, "tp", [(i, i ^ 1) for i in range(8)])
    *lines, dq_own, dq_oth = pl.pallas_call(
        grad_kernel,
        out_shape=(shape((4, SLOTS, 2 * HEAD)),) * 4
        + (
            shape((CHUNKS, ROWS, HEAD), F32),
            shape((CHUNKS, ROWS, HEAD)),
        ),
        in_specs=[pl.BlockSpec(memory_space=pltpu.SMEM)] + whole(8),
        out_specs=tuple(whole(6)),
        scratch_shapes=[
            pltpu.VMEM((PICKED + SLOTS, HEAD), F32),
            pltpu.VMEM((PICKED + SLOTS, HEAD), F32),
            pltpu.VMEM((2 * ROWS, HEAD), F32),
        ],
        compiler_params=params(KERNEL_BYTES),
        cost_estimate=cost(1 << 32),
        name="grads",
    )(info, kc, vc, q_rows, s_rows, comb, raised, pushed, tops)
    delta_near, *lines = lax.optimization_barrier((delta_near, *lines))
    deltas = deltas + delta_near
    lines = lines[:1] + [across(lines[k], k, False) for k in (1, 2, 3)]
    sums = [sum(line[j].astype(F32) for line in lines) for j in range(4)]
    delta_far = lax.ppermute(deltas, "tp", [(i, i ^ 4) for i in range(8)])
    dq_peer = lax.ppermute(dq_oth, "c", swap)
    q_out, closed = pl.pallas_call(
        place_q_kernel,
        out_shape=(shape((TOKENS, GROUP * HEAD)), shape((8, SLOTS), F32)),
        in_specs=whole(4),
        out_specs=tuple(whole(2)),
        compiler_params=params(),
        cost_estimate=cost(1 << 29),
        name="place_q",
    )(picked_row, gate_row, dq_own, dq_peer)
    parts = [sums[j].astype(BF16) for j in (1, 2, 3)]
    delta_far, *parts = lax.optimization_barrier((delta_far, *parts))
    arrived = [across(parts[j - 1], j, True) for j in (1, 2, 3)]
    logit_half = deltas + delta_far
    logit_rest = lax.ppermute(logit_half, "tp", [(i, i ^ 2) for i in range(8)])
    k_out, v_out, logit_out = pl.pallas_call(
        place_kv_kernel,
        out_shape=(
            shape((TOKENS, HEAD)),
            shape((TOKENS, HEAD)),
            shape((TOKENS // SLOTS, SLOTS)),
        ),
        in_specs=whole(8),
        out_specs=tuple(whole(3)),
        compiler_params=params(),
        name="place_kv",
    )(picked_row, closed, sums[0], *arrived, logit_half, logit_rest)
    return q_out, k_out, v_out, logit_out.reshape(TOKENS)


def solution(mesh):
    split = Mesh(mesh.devices.reshape(4, 4, 2, 8), ("y", "x", "c", "tp"))
    seq = ("y", "x", "c")
    return jax.shard_map(
        local,
        mesh=split,
        in_specs=(P(seq, "tp"), P(seq, "tp"), P(seq, "tp"), P(seq), P(seq, "tp"), P(seq)),
        out_specs=(P(seq, "tp"), P(seq, "tp"), P(seq, "tp"), P(seq)),
        check_vma=False,
    )
```

```python
import functools
import math

import jax
import jax.numpy as jnp
from jax import lax
from jax.experimental import pallas as pl
from jax.experimental.pallas import tpu as pltpu
from jax.sharding import Mesh, PartitionSpec as P

QUERY_HEADS = 64
KEY_VALUE_HEADS = 8
HEAD = 128
SLOTS = 128
TOKENS = 512
CHIPS = 16
PICKED = 2048
GROUP = QUERY_HEADS // KEY_VALUE_HEADS
FACTOR = 1.0 / math.sqrt(HEAD)
LOG_FACTOR = FACTOR * math.log2(math.e)
CHUNK = 32
CHUNKS = SLOTS // CHUNK
ROWS = GROUP * CHUNK
KEYS = 512
EDGE = 256
PART = 128
SPARE = 2 * CHUNKS
KEPT = 1536
KERNEL_BYTES = 16 * 1024 * 1024
SENTINEL = 128.0
LIVE_BELOW = 32.0
NEGATIVE = -1e30
F32 = jnp.float32
BF16 = jnp.bfloat16
VMEM_BYTES = 48 * 1024 * 1024
VMEM_ALL = 64 * 1024 * 1024


def nt_dot(a, b):
    return lax.dot_general(a, b, (((1,), (1,)), ((), ())), preferred_element_type=F32)


def tn_dot(a, b):
    return lax.dot_general(a, b, (((0,), (0,)), ((), ())), preferred_element_type=F32)


def place_matrix(picked):
    token = lax.broadcasted_iota(jnp.int32, (TOKENS, SLOTS), 0)
    return jnp.where(token == picked, 1.0, 0.0).astype(F32)


def switch_of(gate, gather):
    rows = jnp.dot(
        jnp.broadcast_to(gate, (16, TOKENS)), gather.astype(BF16), preferred_element_type=F32
    )
    return 1.0 / (1.0 + jnp.exp(-rows))


def fetch(pairs, sems):
    copies = [pltpu.make_async_copy(src, dst, sems.at[n]) for n, (src, dst) in enumerate(pairs)]
    for copy in copies:
        copy.start()
    for copy in copies:
        copy.wait()


def pick_kv_kernel(picked_hbm, k_hbm, v_hbm, kv_out, picked_ref, k_ref, v_ref, message, sems, out_sems):
    pairs = [(picked_hbm, picked_ref), (k_hbm, k_ref), (v_hbm, v_ref)]
    copies = [pltpu.make_async_copy(src, dst, sems.at[n]) for n, (src, dst) in enumerate(pairs)]
    for copy in copies:
        copy.start()
    copies[0].wait()
    column = jnp.broadcast_to(picked_ref[...], (SLOTS, SLOTS)).astype(F32).T
    token = lax.broadcasted_iota(jnp.int32, (SLOTS, SLOTS), 1).astype(F32)
    gather = jnp.concatenate(
        [jnp.where(token + base == column, 1.0, 0.0) for base in range(0, TOKENS, SLOTS)], axis=1
    ).astype(BF16)
    dead = jnp.where(column >= TOKENS, SENTINEL, 0.0)
    copies[1].wait()
    keys = jnp.dot(gather, k_ref[...], preferred_element_type=F32)
    message[:, 0:HEAD] = (keys + dead).astype(BF16)
    copies[2].wait()
    message[:, HEAD : 2 * HEAD] = jnp.dot(
        gather, v_ref[...], preferred_element_type=F32
    ).astype(BF16)
    fetch([(message, kv_out.at[chip]) for chip in range(CHIPS)], out_sems)


def pick_q_kernel(picked_hbm, gate_ref, q_hbm, up_hbm, qs_out, picked_ref, q_ref, up_ref, sems):
    fetch([(picked_hbm, picked_ref), (q_hbm, q_ref), (up_hbm, up_ref)], sems)
    placed = place_matrix(picked_ref[...])
    gather = placed.T.astype(BF16)
    switch = jnp.broadcast_to(switch_of(gate_ref[...], placed)[0:1], (SLOTS, SLOTS)).T
    for h in range(GROUP):
        lanes = slice(h * HEAD, (h + 1) * HEAD)
        q_rows = jnp.dot(gather, q_ref[:, lanes], preferred_element_type=F32).astype(BF16)
        up_rows = jnp.dot(gather, up_ref[:, lanes], preferred_element_type=F32)
        scaled = (up_rows * switch).astype(BF16)
        for t in range(CHUNKS):
            rows = slice(t * CHUNK, (t + 1) * CHUNK)
            qs_out[0, t, h * CHUNK : (h + 1) * CHUNK, :] = q_rows[rows]
            qs_out[1, t, h * CHUNK : (h + 1) * CHUNK, :] = scaled[rows]


def count_live(block):
    live = jnp.where(block.astype(F32) < LIVE_BELOW, 1.0, 0.0)
    return jnp.sum(live, axis=0, keepdims=True)[0, 0].astype(jnp.int32)


class Tiles:
    def __init__(self, core, offset, count, own_chunks, live_chunks):
        self.offset, self.count = offset, count
        self.own_chunks, self.live_chunks = own_chunks, live_chunks
        self.other_limit = offset + jnp.where(core == 0, count, 0)
        self.number = lax.div(live_chunks + 1, 2)

    def place(self, chunk):
        place = jnp.where(chunk < self.own_chunks, chunk, CHUNKS + chunk - self.own_chunks)
        return jnp.where(chunk < self.live_chunks, place, SPARE)

    def limit(self, chunk):
        slot = lax.rem(lax.broadcasted_iota(jnp.int32, (1, ROWS), 1), CHUNK)
        own = self.offset + chunk * CHUNK + 1
        step = jnp.where(chunk < self.own_chunks, 1, 0)
        return jnp.where(chunk < self.own_chunks, own, self.other_limit) + slot * step

    def bounds(self, chunk):
        own = chunk < self.own_chunks
        first = self.offset + chunk * CHUNK
        last = jnp.minimum(first + CHUNK, self.offset + self.count)
        return jnp.where(own, first + 1, self.other_limit), jnp.where(own, last, self.other_limit)

    def spans(self, tile):
        low_a, high_a = self.bounds(2 * tile)
        low_b, high_b = self.bounds(2 * tile + 1)
        paired = 2 * tile + 1 < self.live_chunks
        low = jnp.where(paired, jnp.minimum(low_a, low_b), low_a)
        high = jnp.where(paired, jnp.maximum(high_a, high_b), high_a)
        full = lax.div(low, KEYS)
        rest = high - full * KEYS
        wide = lax.div(rest + EDGE - 1, KEYS)
        return full, wide, rest > wide * KEYS

    def limits(self, tile):
        return jnp.concatenate([self.limit(2 * tile), self.limit(2 * tile + 1)], axis=1)

    def sweep(self, tile, block, carry):
        full, wide, narrow = self.spans(tile)
        limits = self.limits(tile)

        def run(first, count, keys, limits, carry):
            def steps(kept):
                return lambda b, carry: block(
                    pl.multiple_of(first + b * keys, keys), keys, limits, kept, carry
                )

            inside = jnp.minimum(jnp.maximum(lax.div(KEPT - first, keys), 0), count)
            carry = lax.fori_loop(0, inside, steps(True), carry)
            return lax.fori_loop(inside, count, steps(False), carry)

        carry = run(0, full, KEYS, None, carry)
        carry = run(full * KEYS, wide, KEYS, limits, carry)
        last = (full + wide) * KEYS
        return run(last, jnp.where(narrow, 1, 0), EDGE, limits, carry)


def pair_rows(tile):
    return pl.ds(pl.multiple_of(tile * 2 * ROWS, 2 * ROWS), 2 * ROWS)


def stats_kernel(
    peer_picked, kv_ref, own_ref, oth_ref, kc_out, vc_out, q_out, s_out, stats_out, raised_out,
    pushed_out, tops_out, info_out, k_pack, v_pack,
):
    chip = lax.axis_index("y") * 4 + lax.axis_index("x")
    core = lax.axis_index("c")
    stats_out[...] = jnp.zeros_like(stats_out)
    offset = 0
    own_offset = 0
    own_count = 0
    counts = [count_live(kv_ref[s, :, 0:HEAD]) for s in range(CHIPS)]
    for s in range(CHIPS):
        k_pack[pl.ds(offset, SLOTS), :] = kv_ref[s, :, 0:HEAD].astype(F32)
        v_pack[pl.ds(offset, SLOTS), :] = kv_ref[s, :, HEAD : 2 * HEAD].astype(F32)
        info_out[s] = jnp.asarray(offset, jnp.int32)
        own_offset = jnp.where(chip == s, offset, own_offset)
        own_count = jnp.where(chip == s, counts[s], own_count)
        offset = offset + counts[s]
    peer_live = jnp.where(peer_picked[...] < TOKENS, 1.0, 0.0)
    other_count = jnp.sum(peer_live, axis=1, keepdims=True)[0, 0].astype(jnp.int32)
    own_chunks = lax.div(own_count + CHUNK - 1, CHUNK)
    live_chunks = own_chunks + lax.div(other_count + CHUNK - 1, CHUNK)
    info_out[16] = own_offset
    info_out[17] = own_count
    info_out[18] = own_chunks
    info_out[19] = live_chunks
    tail = pl.ds(offset + SLOTS, KEYS)
    k_pack[tail, :] = jnp.zeros((KEYS, HEAD), F32)
    v_pack[tail, :] = jnp.zeros((KEYS, HEAD), F32)

    def narrow_keys(b, _):
        rows = pl.ds(pl.multiple_of(b * KEYS, KEYS), KEYS)
        kc_out[rows, :] = k_pack[rows, :].astype(BF16)
        vc_out[rows, :] = v_pack[rows, :].astype(BF16)
        return 0

    lax.fori_loop(0, lax.div(own_offset + own_count + KEYS - 1, KEYS), narrow_keys, 0)
    for t in range(CHUNKS):
        q_out[t * ROWS : (t + 1) * ROWS, :] = own_ref[0, t]
        s_out[t * ROWS : (t + 1) * ROWS, :] = own_ref[1, t]
    for t in range(CHUNKS):
        rows = pl.ds(pl.multiple_of((own_chunks + t) * ROWS, ROWS), ROWS)
        q_out[rows, :] = oth_ref[0, t]
        s_out[rows, :] = oth_ref[1, t]
    spare = pl.ds(pl.multiple_of(live_chunks * ROWS, ROWS), ROWS)
    q_out[spare, :] = jnp.zeros((ROWS, HEAD), BF16)
    s_out[spare, :] = jnp.zeros((ROWS, HEAD), BF16)
    tiles = Tiles(core, own_offset, own_count, own_chunks, live_chunks)

    def attend(tile, _):
        q_rows = q_out[pair_rows(tile), :]
        s_rows = s_out[pair_rows(tile), :]

        def block(base, keys, limits, kept, carry):
            top, total, pull = carry
            scores = nt_dot(kc_out[pl.ds(base, keys), :], q_rows)
            pushed = nt_dot(vc_out[pl.ds(base, keys), :], s_rows)
            if kept:
                pushed_out[tile, pl.ds(base, keys), :] = pushed
            for u in range(0, keys, PART):
                part = scores[u : u + PART] * LOG_FACTOR
                if limits is not None:
                    index = lax.broadcasted_iota(jnp.int32, (PART, 2 * ROWS), 0)
                    part = jnp.where(index < limits - (base + u), part, NEGATIVE)
                part = part.reshape(PART // 8, 8, 2 * ROWS)
                new_top = jnp.maximum(top, jnp.max(part, axis=0))
                raised = jnp.exp2(part - new_top[None])
                if kept:
                    rows = pl.ds(pl.multiple_of(base + u, PART), PART)
                    raised_out[tile, rows, :] = raised.reshape(PART, 2 * ROWS)
                    tops_out[tile, lax.div(base + u, PART)] = new_top
                fade = jnp.exp2(top - new_top)
                total = total * fade + jnp.sum(raised, axis=0)
                pulled = raised * pushed[u : u + PART].reshape(PART // 8, 8, 2 * ROWS)
                pull = pull * fade + jnp.sum(pulled, axis=0)
                top = new_top
            return top, total, pull

        zero = jnp.zeros((8, 2 * ROWS), F32)
        top, total, pull = tiles.sweep(
            tile, block, (jnp.full((8, 2 * ROWS), NEGATIVE, F32), zero, zero)
        )
        best = jnp.max(top, axis=0, keepdims=True)
        fade = jnp.exp2(top - best)
        total = jnp.sum(total * fade, axis=0, keepdims=True)
        pull = jnp.sum(pull * fade, axis=0, keepdims=True)
        for half in range(2):
            place = tiles.place(2 * tile + half)
            lanes = slice(half * ROWS, (half + 1) * ROWS)
            stats_out[place, 0:1, :] = best[:, lanes]
            stats_out[place, 1:2, :] = total[:, lanes]
            stats_out[place, 2:3, :] = pull[:, lanes]
        return 0

    lax.fori_loop(0, tiles.number, attend, 0)


def combine_kernel(info_ref, stats_ref, peer_ref, comb_out, delta_out):
    own_chunks = info_ref[18]

    def of(ref, kind, swap):
        first, second = ref[0:CHUNKS, kind, :], ref[CHUNKS:SPARE, kind, :]
        return jnp.concatenate([second, first] if swap else [first, second], axis=0)

    top_a, top_b = of(stats_ref, 0, False), of(peer_ref, 0, True)
    top = jnp.maximum(top_a, top_b)
    scale_a, scale_b = jnp.exp2(top_a - top), jnp.exp2(top_b - top)
    total = of(stats_ref, 1, False) * scale_a + of(peer_ref, 1, True) * scale_b
    total = jnp.where(total > 0.0, total, 1.0)
    delta = (of(stats_ref, 2, False) * scale_a + of(peer_ref, 2, True) * scale_b) / total
    comb_out[...] = jnp.zeros_like(comb_out)
    comb_out[0:SPARE, 0, :] = top + jnp.log2(total)
    comb_out[0:SPARE, 1, :] = delta
    heads = delta[:, 0:128] + delta[:, 128:256]
    heads = heads + pltpu.roll(heads, 64, 1)
    heads = heads + pltpu.roll(heads, 32, 1)
    lane = lax.div(lax.broadcasted_iota(jnp.int32, (SPARE, SLOTS), 1), CHUNK)
    chunk = lax.broadcasted_iota(jnp.int32, (SPARE, SLOTS), 0)
    heads = jnp.where((lane == chunk) & (chunk < own_chunks), heads, 0.0)
    deltas = jnp.sum(heads, axis=0, keepdims=True)
    delta_out[...] = jnp.broadcast_to(deltas, (8, SLOTS))


def grad_kernel(
    info_ref, kc_ref, vc_ref, q_ref, s_ref, comb_ref, raised_ref, pushed_ref, tops_ref,
    line_0, line_1, line_2, line_3, dq_own, dq_oth, dk_sum, dv_sum, dq_sum,
):
    core = lax.axis_index("c")
    tiles = Tiles(core, info_ref[16], info_ref[17], info_ref[18], info_ref[19])
    dk_sum[...] = jnp.zeros_like(dk_sum)
    dv_sum[...] = jnp.zeros_like(dv_sum)
    dq_own[...] = jnp.zeros_like(dq_own)
    dq_oth[...] = jnp.zeros_like(dq_oth)

    def push_back(tile, _):
        q_rows = q_ref[pair_rows(tile), :]
        s_rows = s_ref[pair_rows(tile), :]
        chunks = (2 * tile, 2 * tile + 1)
        comb = jnp.concatenate([comb_ref[tiles.place(c)] for c in chunks], axis=1)
        level, delta = comb[0:1], comb[1:2]
        dq_sum[...] = jnp.zeros_like(dq_sum)

        def block(base, keys, limits, kept, carry):
            span = pl.ds(base, keys)
            key_rows = kc_ref[span, :]
            if kept:
                pushed = pushed_ref[tile, span, :]
                parts = []
                for u in range(0, keys, PART):
                    rows = pl.ds(pl.multiple_of(base + u, PART), PART)
                    scale = jnp.exp2(tops_ref[tile, lax.div(base + u, PART)] - level)
                    part = raised_ref[tile, rows, :].reshape(PART // 8, 8, 2 * ROWS)
                    parts.append((part * scale[None]).reshape(PART, 2 * ROWS))
                weights = jnp.concatenate(parts, axis=0)
            else:
                scores = nt_dot(key_rows, q_rows)
                pushed = nt_dot(vc_ref[span, :], s_rows)
                weights = jnp.exp2(scores * LOG_FACTOR - level)
                if limits is not None:
                    index = lax.broadcasted_iota(jnp.int32, (keys, 2 * ROWS), 0)
                    weights = jnp.where(index < limits - base, weights, 0.0)
            slopes = (weights * (pushed - delta)).astype(BF16)
            dv_sum[span, :] += jnp.dot(
                weights.astype(BF16), s_rows, preferred_element_type=F32
            )
            dk_sum[span, :] += jnp.dot(slopes, q_rows, preferred_element_type=F32)
            dq_sum[...] += tn_dot(slopes, key_rows)
            return carry

        tiles.sweep(tile, block, 0)
        for half, chunk in enumerate(chunks):
            rows = slice(half * ROWS, (half + 1) * ROWS)

            @pl.when(chunk < tiles.own_chunks)
            def _():
                dq_own[chunk] = dq_sum[rows, :]

            @pl.when((chunk >= tiles.own_chunks) & (chunk < tiles.live_chunks))
            def _():
                dq_oth[chunk - tiles.own_chunks] = dq_sum[rows, :].astype(BF16)

        return 0

    lax.fori_loop(0, tiles.number, push_back, 0)
    row, column = lax.axis_index("y"), lax.axis_index("x")
    for k, line in enumerate((line_0, line_1, line_2, line_3)):
        for j in range(4):
            down, right = jnp.where(core == 0, k, j), jnp.where(core == 0, j, k)
            chip = lax.rem(row + down, 4) * 4 + lax.rem(column + right, 4)
            rows = pl.ds(info_ref[chip], SLOTS)
            line[j, :, 0:HEAD] = dk_sum[rows, :].astype(BF16)
            line[j, :, HEAD : 2 * HEAD] = dv_sum[rows, :].astype(BF16)


def place_q_kernel(picked_ref, gate_ref, dq_own, dq_peer, q_out, closed_out):
    placed = place_matrix(picked_ref[...])
    scatter = placed.astype(BF16)
    closed_out[...] = 1.0 - switch_of(gate_ref[...], placed)[0:8]
    for h in range(GROUP):
        rows = slice(h * CHUNK, (h + 1) * CHUNK)
        parts = [
            ((dq_own[t, rows, :] + dq_peer[t, rows, :].astype(F32)) * FACTOR).astype(BF16)
            for t in range(CHUNKS)
        ]
        q_out[:, h * HEAD : (h + 1) * HEAD] = jnp.dot(
            scatter, jnp.concatenate(parts, axis=0), preferred_element_type=F32
        ).astype(BF16)


def place_kv_kernel(
    picked_ref, closed_ref, own_ref, sum_1, sum_2, sum_3, part_a, part_b, k_out, v_out, logit_out
):
    scatter = place_matrix(picked_ref[...]).astype(BF16)
    total = own_ref[...]
    for other in (sum_1, sum_2, sum_3):
        total = total + other[...].astype(F32)
    k_rows = (total[:, 0:HEAD] * FACTOR).astype(BF16)
    v_rows = total[:, HEAD : 2 * HEAD].astype(BF16)
    k_out[...] = jnp.dot(scatter, k_rows, preferred_element_type=F32).astype(BF16)
    v_out[...] = jnp.dot(scatter, v_rows, preferred_element_type=F32).astype(BF16)
    logits = (part_a[...] + part_b[...]) * closed_ref[...]
    logit_rows = jnp.concatenate([logits, logits], axis=0).astype(BF16)
    for part in range(TOKENS // SLOTS):
        rows = slice(part * SLOTS, (part + 1) * SLOTS)
        logit_out[part : part + 1, :] = nt_dot(logit_rows, scatter[rows])[0:1].astype(BF16)


def whole(count):
    return [pl.BlockSpec(memory_space=pltpu.VMEM)] * count


def params(limit=VMEM_BYTES):
    return pltpu.CompilerParams(vmem_limit_bytes=limit)


def shape(dims, kind=BF16):
    return jax.ShapeDtypeStruct(dims, kind)


def hbm(count):
    return [pl.BlockSpec(memory_space=pltpu.HBM)] * count


def cost(flops):
    return pl.CostEstimate(flops=flops, bytes_accessed=1 << 20, transcendentals=0)


def across(block, step, first):
    def device(y, x, c):
        return (y % 4 * 4 + x % 4) * 2 + c

    pairs = []
    for y in range(4):
        for x in range(4):
            for c in range(2):
                along_x = (c == 0) == first
                target = device(y, x + step, c) if along_x else device(y + step, x, c)
                pairs.append((device(y, x, c), target))
    return lax.ppermute(block, ("y", "x", "c"), pairs)


def local(head_queries, key_projection_rows, value_projection_rows, gate_logit, upstream, picked):
    picked_row = picked.reshape(1, SLOTS)
    swap = [(0, 1), (1, 0)]
    kv_copies = pl.pallas_call(
        pick_kv_kernel,
        out_shape=shape((CHIPS, SLOTS, 2 * HEAD)),
        in_specs=hbm(3),
        out_specs=hbm(1)[0],
        scratch_shapes=[
            pltpu.VMEM((1, SLOTS), jnp.int32),
            pltpu.VMEM((TOKENS, HEAD), BF16),
            pltpu.VMEM((TOKENS, HEAD), BF16),
            pltpu.VMEM((SLOTS, 2 * HEAD), BF16),
            pltpu.SemaphoreType.DMA((3,)),
            pltpu.SemaphoreType.DMA((CHIPS,)),
        ],
        compiler_params=params(VMEM_ALL),
        name="pick_kv",
    )(picked_row, key_projection_rows, value_projection_rows)
    kv_all = lax.all_to_all(kv_copies, ("y", "x"), 0, 0, tiled=True)
    gate_row = gate_logit.reshape(1, TOKENS)
    qs_own = pl.pallas_call(
        pick_q_kernel,
        out_shape=shape((2, CHUNKS, ROWS, HEAD)),
        in_specs=hbm(1) + whole(1) + hbm(2),
        out_specs=whole(1)[0],
        scratch_shapes=[
            pltpu.VMEM((1, SLOTS), jnp.int32),
            pltpu.VMEM((TOKENS, GROUP * HEAD), BF16),
            pltpu.VMEM((TOKENS, GROUP * HEAD), BF16),
            pltpu.SemaphoreType.DMA((3,)),
        ],
        compiler_params=params(),
        cost_estimate=cost(1 << 30),
        name="pick_q",
    )(picked_row, gate_row, head_queries, upstream)
    qs_peer = lax.ppermute(qs_own, "c", swap)
    peer_picked = lax.ppermute(picked_row, "c", swap)
    kc, vc, q_rows, s_rows, stats, raised, pushed, tops, info = pl.pallas_call(
        stats_kernel,
        out_shape=(
            shape((PICKED, HEAD)),
            shape((PICKED, HEAD)),
            shape(((2 * CHUNKS + 1) * ROWS, HEAD)),
            shape(((2 * CHUNKS + 1) * ROWS, HEAD)),
            shape((SPARE + 1, 8, ROWS), F32),
            shape((CHUNKS, KEPT, 2 * ROWS), F32),
            shape((CHUNKS, KEPT, 2 * ROWS), F32),
            shape((CHUNKS, KEPT // PART, 8, 2 * ROWS), F32),
            shape((32,), jnp.int32),
        ),
        in_specs=whole(4),
        out_specs=tuple(whole(8)) + (pl.BlockSpec(memory_space=pltpu.SMEM),),
        scratch_shapes=[pltpu.VMEM((PICKED + SLOTS + KEYS, HEAD), F32)] * 2,
        compiler_params=params(KERNEL_BYTES),
        name="stats",
    )(peer_picked, kv_all, qs_own, qs_peer)
    stats_peer = lax.ppermute(stats, "c", swap)
    comb, deltas = pl.pallas_call(
        combine_kernel,
        out_shape=(shape((SPARE + 1, 8, ROWS), F32), shape((8, SLOTS), F32)),
        in_specs=[pl.BlockSpec(memory_space=pltpu.SMEM)] + whole(2),
        out_specs=tuple(whole(2)),
        compiler_params=params(KERNEL_BYTES),
        name="combine",
    )(info, stats, stats_peer)
    delta_near = lax.ppermute(deltas, "tp", [(i, i ^ 1) for i in range(8)])
    *lines, dq_own, dq_oth = pl.pallas_call(
        grad_kernel,
        out_shape=(shape((4, SLOTS, 2 * HEAD)),) * 4
        + (
            shape((CHUNKS, ROWS, HEAD), F32),
            shape((CHUNKS, ROWS, HEAD)),
        ),
        in_specs=[pl.BlockSpec(memory_space=pltpu.SMEM)] + whole(8),
        out_specs=tuple(whole(6)),
        scratch_shapes=[
            pltpu.VMEM((PICKED + SLOTS, HEAD), F32),
            pltpu.VMEM((PICKED + SLOTS, HEAD), F32),
            pltpu.VMEM((2 * ROWS, HEAD), F32),
        ],
        compiler_params=params(KERNEL_BYTES),
        cost_estimate=cost(1 << 32),
        name="grads",
    )(info, kc, vc, q_rows, s_rows, comb, raised, pushed, tops)
    delta_near, *lines = lax.optimization_barrier((delta_near, *lines))
    deltas = deltas + delta_near
    moved = {k: across(lines[k], k, False) for k in (2, 3, 1)}
    lines = lines[:1] + [moved[k] for k in (1, 2, 3)]
    sums = [sum(line[j].astype(F32) for line in lines) for j in range(4)]
    delta_far = lax.ppermute(deltas, "tp", [(i, i ^ 4) for i in range(8)])
    dq_peer = lax.ppermute(dq_oth, "c", swap)
    q_out, closed = pl.pallas_call(
        place_q_kernel,
        out_shape=(shape((TOKENS, GROUP * HEAD)), shape((8, SLOTS), F32)),
        in_specs=whole(4),
        out_specs=tuple(whole(2)),
        compiler_params=params(),
        cost_estimate=cost(1 << 29),
        name="place_q",
    )(picked_row, gate_row, dq_own, dq_peer)
    parts = [sums[j].astype(BF16) for j in (1, 2, 3)]
    delta_far, *parts = lax.optimization_barrier((delta_far, *parts))
    arrived = [across(parts[j - 1], j, True) for j in (1, 2, 3)]
    logit_half = deltas + delta_far
    logit_rest = lax.ppermute(logit_half, "tp", [(i, i ^ 2) for i in range(8)])
    k_out, v_out, logit_out = pl.pallas_call(
        place_kv_kernel,
        out_shape=(
            shape((TOKENS, HEAD)),
            shape((TOKENS, HEAD)),
            shape((TOKENS // SLOTS, SLOTS)),
        ),
        in_specs=whole(8),
        out_specs=tuple(whole(3)),
        compiler_params=params(),
        name="place_kv",
    )(picked_row, closed, sums[0], *arrived, logit_half, logit_rest)
    return q_out, k_out, v_out, logit_out.reshape(TOKENS)


def solution(mesh):
    split = Mesh(mesh.devices.reshape(4, 4, 2, 8), ("y", "x", "c", "tp"))
    seq = ("y", "x", "c")
    return jax.shard_map(
        local,
        mesh=split,
        in_specs=(P(seq, "tp"), P(seq, "tp"), P(seq, "tp"), P(seq), P(seq, "tp"), P(seq)),
        out_specs=(P(seq, "tp"), P(seq, "tp"), P(seq, "tp"), P(seq)),
        check_vma=False,
    )
```

```python
import functools
import math

import jax
import jax.numpy as jnp
from jax import lax
from jax.experimental import pallas as pl
from jax.experimental.pallas import tpu as pltpu
from jax.sharding import Mesh, PartitionSpec as P

QUERY_HEADS = 64
KEY_VALUE_HEADS = 8
HEAD = 128
SLOTS = 128
TOKENS = 512
CHIPS = 16
PICKED = 2048
GROUP = QUERY_HEADS // KEY_VALUE_HEADS
FACTOR = 1.0 / math.sqrt(HEAD)
LOG_FACTOR = FACTOR * math.log2(math.e)
CHUNK = 32
CHUNKS = SLOTS // CHUNK
ROWS = GROUP * CHUNK
KEYS = 512
EDGE = 256
PART = 256
SPARE = 2 * CHUNKS
KEPT = 1536
KERNEL_BYTES = 16 * 1024 * 1024
SENTINEL = 128.0
LIVE_BELOW = 32.0
NEGATIVE = -1e30
F32 = jnp.float32
BF16 = jnp.bfloat16
VMEM_BYTES = 48 * 1024 * 1024
VMEM_ALL = 64 * 1024 * 1024


def nt_dot(a, b):
    return lax.dot_general(a, b, (((1,), (1,)), ((), ())), preferred_element_type=F32)


def tn_dot(a, b):
    return lax.dot_general(a, b, (((0,), (0,)), ((), ())), preferred_element_type=F32)


def place_matrix(picked):
    token = lax.broadcasted_iota(jnp.int32, (TOKENS, SLOTS), 0)
    return jnp.where(token == picked, 1.0, 0.0).astype(F32)


def switch_of(gate, gather):
    rows = jnp.dot(
        jnp.broadcast_to(gate, (16, TOKENS)), gather.astype(BF16), preferred_element_type=F32
    )
    return 1.0 / (1.0 + jnp.exp(-rows))


def fetch(pairs, sems):
    copies = [pltpu.make_async_copy(src, dst, sems.at[n]) for n, (src, dst) in enumerate(pairs)]
    for copy in copies:
        copy.start()
    for copy in copies:
        copy.wait()


def pick_kv_kernel(picked_hbm, k_hbm, v_hbm, kv_out, picked_ref, k_ref, v_ref, message, sems, out_sems):
    pairs = [(picked_hbm, picked_ref), (k_hbm, k_ref), (v_hbm, v_ref)]
    copies = [pltpu.make_async_copy(src, dst, sems.at[n]) for n, (src, dst) in enumerate(pairs)]
    for copy in copies:
        copy.start()
    copies[0].wait()
    column = jnp.broadcast_to(picked_ref[...], (SLOTS, SLOTS)).astype(F32).T
    token = lax.broadcasted_iota(jnp.int32, (SLOTS, SLOTS), 1).astype(F32)
    gather = jnp.concatenate(
        [jnp.where(token + base == column, 1.0, 0.0) for base in range(0, TOKENS, SLOTS)], axis=1
    ).astype(BF16)
    dead = jnp.where(column >= TOKENS, SENTINEL, 0.0)
    copies[1].wait()
    keys = jnp.dot(gather, k_ref[...], preferred_element_type=F32)
    message[:, 0:HEAD] = (keys + dead).astype(BF16)
    copies[2].wait()
    message[:, HEAD : 2 * HEAD] = jnp.dot(
        gather, v_ref[...], preferred_element_type=F32
    ).astype(BF16)
    fetch([(message, kv_out.at[chip]) for chip in range(CHIPS)], out_sems)


def pick_q_kernel(picked_hbm, gate_ref, q_hbm, up_hbm, qs_out, picked_ref, q_ref, up_ref, sems):
    fetch([(picked_hbm, picked_ref), (q_hbm, q_ref), (up_hbm, up_ref)], sems)
    placed = place_matrix(picked_ref[...])
    gather = placed.T.astype(BF16)
    switch = jnp.broadcast_to(switch_of(gate_ref[...], placed)[0:1], (SLOTS, SLOTS)).T
    for h in range(GROUP):
        lanes = slice(h * HEAD, (h + 1) * HEAD)
        q_rows = jnp.dot(gather, q_ref[:, lanes], preferred_element_type=F32).astype(BF16)
        up_rows = jnp.dot(gather, up_ref[:, lanes], preferred_element_type=F32)
        scaled = (up_rows * switch).astype(BF16)
        for t in range(CHUNKS):
            rows = slice(t * CHUNK, (t + 1) * CHUNK)
            qs_out[0, t, h * CHUNK : (h + 1) * CHUNK, :] = q_rows[rows]
            qs_out[1, t, h * CHUNK : (h + 1) * CHUNK, :] = scaled[rows]


def count_live(block):
    live = jnp.where(block.astype(F32) < LIVE_BELOW, 1.0, 0.0)
    return jnp.sum(live, axis=0, keepdims=True)[0, 0].astype(jnp.int32)


class Tiles:
    def __init__(self, core, offset, count, own_chunks, live_chunks):
        self.offset, self.count = offset, count
        self.own_chunks, self.live_chunks = own_chunks, live_chunks
        self.other_limit = offset + jnp.where(core == 0, count, 0)
        self.number = lax.div(live_chunks + 1, 2)

    def place(self, chunk):
        place = jnp.where(chunk < self.own_chunks, chunk, CHUNKS + chunk - self.own_chunks)
        return jnp.where(chunk < self.live_chunks, place, SPARE)

    def limit(self, chunk):
        slot = lax.rem(lax.broadcasted_iota(jnp.int32, (1, ROWS), 1), CHUNK)
        own = self.offset + chunk * CHUNK + 1
        step = jnp.where(chunk < self.own_chunks, 1, 0)
        return jnp.where(chunk < self.own_chunks, own, self.other_limit) + slot * step

    def bounds(self, chunk):
        own = chunk < self.own_chunks
        first = self.offset + chunk * CHUNK
        last = jnp.minimum(first + CHUNK, self.offset + self.count)
        return jnp.where(own, first + 1, self.other_limit), jnp.where(own, last, self.other_limit)

    def spans(self, tile):
        low_a, high_a = self.bounds(2 * tile)
        low_b, high_b = self.bounds(2 * tile + 1)
        paired = 2 * tile + 1 < self.live_chunks
        low = jnp.where(paired, jnp.minimum(low_a, low_b), low_a)
        high = jnp.where(paired, jnp.maximum(high_a, high_b), high_a)
        full = lax.div(low, KEYS)
        rest = high - full * KEYS
        wide = lax.div(rest + EDGE - 1, KEYS)
        return full, wide, rest > wide * KEYS

    def limits(self, tile):
        return jnp.concatenate([self.limit(2 * tile), self.limit(2 * tile + 1)], axis=1)

    def sweep(self, tile, block, carry):
        full, wide, narrow = self.spans(tile)
        limits = self.limits(tile)

        def run(first, count, keys, limits, carry):
            def steps(kept):
                return lambda b, carry: block(
                    pl.multiple_of(first + b * keys, keys), keys, limits, kept, carry
                )

            inside = jnp.minimum(jnp.maximum(lax.div(KEPT - first, keys), 0), count)
            carry = lax.fori_loop(0, inside, steps(True), carry)
            return lax.fori_loop(inside, count, steps(False), carry)

        carry = run(0, full, KEYS, None, carry)
        carry = run(full * KEYS, wide, KEYS, limits, carry)
        last = (full + wide) * KEYS
        return run(last, jnp.where(narrow, 1, 0), EDGE, limits, carry)


def pair_rows(tile):
    return pl.ds(pl.multiple_of(tile * 2 * ROWS, 2 * ROWS), 2 * ROWS)


def stats_kernel(
    peer_picked, kv_ref, own_ref, oth_ref, kc_out, vc_out, q_out, s_out, stats_out, raised_out,
    pushed_out, tops_out, info_out, k_pack, v_pack,
):
    chip = lax.axis_index("y") * 4 + lax.axis_index("x")
    core = lax.axis_index("c")
    stats_out[...] = jnp.zeros_like(stats_out)
    offset = 0
    own_offset = 0
    own_count = 0
    counts = [count_live(kv_ref[s, :, 0:HEAD]) for s in range(CHIPS)]
    for s in range(CHIPS):
        k_pack[pl.ds(offset, SLOTS), :] = kv_ref[s, :, 0:HEAD].astype(F32)
        v_pack[pl.ds(offset, SLOTS), :] = kv_ref[s, :, HEAD : 2 * HEAD].astype(F32)
        info_out[s] = jnp.asarray(offset, jnp.int32)
        own_offset = jnp.where(chip == s, offset, own_offset)
        own_count = jnp.where(chip == s, counts[s], own_count)
        offset = offset + counts[s]
    peer_live = jnp.where(peer_picked[...] < TOKENS, 1.0, 0.0)
    other_count = jnp.sum(peer_live, axis=1, keepdims=True)[0, 0].astype(jnp.int32)
    own_chunks = lax.div(own_count + CHUNK - 1, CHUNK)
    live_chunks = own_chunks + lax.div(other_count + CHUNK - 1, CHUNK)
    info_out[16] = own_offset
    info_out[17] = own_count
    info_out[18] = own_chunks
    info_out[19] = live_chunks
    tail = pl.ds(offset + SLOTS, KEYS)
    k_pack[tail, :] = jnp.zeros((KEYS, HEAD), F32)
    v_pack[tail, :] = jnp.zeros((KEYS, HEAD), F32)

    def narrow_keys(b, _):
        rows = pl.ds(pl.multiple_of(b * KEYS, KEYS), KEYS)
        kc_out[rows, :] = k_pack[rows, :].astype(BF16)
        vc_out[rows, :] = v_pack[rows, :].astype(BF16)
        return 0

    lax.fori_loop(0, lax.div(own_offset + own_count + KEYS - 1, KEYS), narrow_keys, 0)
    for t in range(CHUNKS):
        q_out[t * ROWS : (t + 1) * ROWS, :] = own_ref[0, t]
        s_out[t * ROWS : (t + 1) * ROWS, :] = own_ref[1, t]
    for t in range(CHUNKS):
        rows = pl.ds(pl.multiple_of((own_chunks + t) * ROWS, ROWS), ROWS)
        q_out[rows, :] = oth_ref[0, t]
        s_out[rows, :] = oth_ref[1, t]
    spare = pl.ds(pl.multiple_of(live_chunks * ROWS, ROWS), ROWS)
    q_out[spare, :] = jnp.zeros((ROWS, HEAD), BF16)
    s_out[spare, :] = jnp.zeros((ROWS, HEAD), BF16)
    tiles = Tiles(core, own_offset, own_count, own_chunks, live_chunks)

    def attend(tile, _):
        q_rows = q_out[pair_rows(tile), :]
        s_rows = s_out[pair_rows(tile), :]

        def block(base, keys, limits, kept, carry):
            top, total, pull = carry
            scores = nt_dot(kc_out[pl.ds(base, keys), :], q_rows)
            pushed = nt_dot(vc_out[pl.ds(base, keys), :], s_rows)
            if kept:
                pushed_out[tile, pl.ds(base, keys), :] = pushed
            for u in range(0, keys, PART):
                part = scores[u : u + PART] * LOG_FACTOR
                if limits is not None:
                    index = lax.broadcasted_iota(jnp.int32, (PART, 2 * ROWS), 0)
                    part = jnp.where(index < limits - (base + u), part, NEGATIVE)
                part = part.reshape(PART // 8, 8, 2 * ROWS)
                new_top = jnp.maximum(top, jnp.max(part, axis=0))
                raised = jnp.exp2(part - new_top[None])
                if kept:
                    rows = pl.ds(pl.multiple_of(base + u, PART), PART)
                    raised_out[tile, rows, :] = raised.reshape(PART, 2 * ROWS)
                    tops_out[tile, lax.div(base + u, PART)] = new_top
                fade = jnp.exp2(top - new_top)
                total = total * fade + jnp.sum(raised, axis=0)
                pulled = raised * pushed[u : u + PART].reshape(PART // 8, 8, 2 * ROWS)
                pull = pull * fade + jnp.sum(pulled, axis=0)
                top = new_top
            return top, total, pull

        zero = jnp.zeros((8, 2 * ROWS), F32)
        top, total, pull = tiles.sweep(
            tile, block, (jnp.full((8, 2 * ROWS), NEGATIVE, F32), zero, zero)
        )
        best = jnp.max(top, axis=0, keepdims=True)
        fade = jnp.exp2(top - best)
        total = jnp.sum(total * fade, axis=0, keepdims=True)
        pull = jnp.sum(pull * fade, axis=0, keepdims=True)
        for half in range(2):
            place = tiles.place(2 * tile + half)
            lanes = slice(half * ROWS, (half + 1) * ROWS)
            stats_out[place, 0:1, :] = best[:, lanes]
            stats_out[place, 1:2, :] = total[:, lanes]
            stats_out[place, 2:3, :] = pull[:, lanes]
        return 0

    lax.fori_loop(0, tiles.number, attend, 0)


def combine_kernel(info_ref, stats_ref, peer_ref, comb_out, delta_out):
    own_chunks = info_ref[18]
    lane = lax.div(lax.broadcasted_iota(jnp.int32, (1, SLOTS), 1), CHUNK)
    comb_out[SPARE] = jnp.zeros((8, ROWS), F32)
    deltas = jnp.zeros((1, SLOTS), F32)
    for place in range(SPARE):
        mine = stats_ref[place]
        theirs = peer_ref[(place + CHUNKS) % SPARE]
        top = jnp.maximum(mine[0:1], theirs[0:1])
        mine_scale = jnp.exp2(mine[0:1] - top)
        their_scale = jnp.exp2(theirs[0:1] - top)
        total = mine[1:2] * mine_scale + theirs[1:2] * their_scale
        total = jnp.where(total > 0.0, total, 1.0)
        delta = (mine[2:3] * mine_scale + theirs[2:3] * their_scale) / total
        comb_out[place, 0:1, :] = top + jnp.log2(total)
        comb_out[place, 1:2, :] = delta
        if place < CHUNKS:
            heads = delta[:, 0:128] + delta[:, 128:256]
            heads = heads + pltpu.roll(heads, 64, 1)
            heads = heads + pltpu.roll(heads, 32, 1)
            mark = jnp.where(place < own_chunks, place, CHUNKS)
            deltas = deltas + jnp.where(lane == mark, heads, 0.0)
    delta_out[...] = jnp.broadcast_to(deltas, (8, SLOTS))


def grad_kernel(
    info_ref, kc_ref, vc_ref, q_ref, s_ref, comb_ref, raised_ref, pushed_ref, tops_ref,
    line_0, line_1, line_2, line_3, dq_own, dq_oth, dk_sum, dv_sum, dq_sum,
):
    core = lax.axis_index("c")
    tiles = Tiles(core, info_ref[16], info_ref[17], info_ref[18], info_ref[19])
    dk_sum[...] = jnp.zeros_like(dk_sum)
    dv_sum[...] = jnp.zeros_like(dv_sum)
    dq_own[...] = jnp.zeros_like(dq_own)
    dq_oth[...] = jnp.zeros_like(dq_oth)

    def push_back(tile, _):
        q_rows = q_ref[pair_rows(tile), :]
        s_rows = s_ref[pair_rows(tile), :]
        chunks = (2 * tile, 2 * tile + 1)
        comb = jnp.concatenate([comb_ref[tiles.place(c)] for c in chunks], axis=1)
        level, delta = comb[0:1], comb[1:2]
        dq_sum[...] = jnp.zeros_like(dq_sum)

        def block(base, keys, limits, kept, carry):
            span = pl.ds(base, keys)
            key_rows = kc_ref[span, :]
            if kept:
                pushed = pushed_ref[tile, span, :]
                parts = []
                for u in range(0, keys, PART):
                    rows = pl.ds(pl.multiple_of(base + u, PART), PART)
                    scale = jnp.exp2(tops_ref[tile, lax.div(base + u, PART)] - level)
                    part = raised_ref[tile, rows, :].reshape(PART // 8, 8, 2 * ROWS)
                    parts.append((part * scale[None]).reshape(PART, 2 * ROWS))
                weights = jnp.concatenate(parts, axis=0)
            else:
                scores = nt_dot(key_rows, q_rows)
                pushed = nt_dot(vc_ref[span, :], s_rows)
                weights = jnp.exp2(scores * LOG_FACTOR - level)
                if limits is not None:
                    index = lax.broadcasted_iota(jnp.int32, (keys, 2 * ROWS), 0)
                    weights = jnp.where(index < limits - base, weights, 0.0)
            slopes = (weights * (pushed - delta)).astype(BF16)
            dv_sum[span, :] += jnp.dot(
                weights.astype(BF16), s_rows, preferred_element_type=F32
            )
            dk_sum[span, :] += jnp.dot(slopes, q_rows, preferred_element_type=F32)
            dq_sum[...] += tn_dot(slopes, key_rows)
            return carry

        tiles.sweep(tile, block, 0)
        for half, chunk in enumerate(chunks):
            rows = slice(half * ROWS, (half + 1) * ROWS)

            @pl.when(chunk < tiles.own_chunks)
            def _():
                dq_own[chunk] = dq_sum[rows, :]

            @pl.when((chunk >= tiles.own_chunks) & (chunk < tiles.live_chunks))
            def _():
                dq_oth[chunk - tiles.own_chunks] = dq_sum[rows, :].astype(BF16)

        return 0

    lax.fori_loop(0, tiles.number, push_back, 0)
    row, column = lax.axis_index("y"), lax.axis_index("x")
    for k, line in enumerate((line_0, line_1, line_2, line_3)):
        for j in range(4):
            down, right = jnp.where(core == 0, k, j), jnp.where(core == 0, j, k)
            chip = lax.rem(row + down, 4) * 4 + lax.rem(column + right, 4)
            rows = pl.ds(info_ref[chip], SLOTS)
            line[j, :, 0:HEAD] = dk_sum[rows, :].astype(BF16)
            line[j, :, HEAD : 2 * HEAD] = dv_sum[rows, :].astype(BF16)


def place_q_kernel(picked_ref, gate_ref, dq_own, dq_peer, q_out, closed_out):
    placed = place_matrix(picked_ref[...])
    scatter = placed.astype(BF16)
    closed_out[...] = 1.0 - switch_of(gate_ref[...], placed)[0:8]
    for h in range(GROUP):
        rows = slice(h * CHUNK, (h + 1) * CHUNK)
        parts = [
            ((dq_own[t, rows, :] + dq_peer[t, rows, :].astype(F32)) * FACTOR).astype(BF16)
            for t in range(CHUNKS)
        ]
        q_out[:, h * HEAD : (h + 1) * HEAD] = jnp.dot(
            scatter, jnp.concatenate(parts, axis=0), preferred_element_type=F32
        ).astype(BF16)


def place_kv_kernel(
    picked_ref, closed_ref, own_ref, sum_1, sum_2, sum_3, part_a, part_b, k_out, v_out, logit_out
):
    scatter = place_matrix(picked_ref[...]).astype(BF16)
    total = own_ref[...]
    for other in (sum_1, sum_2, sum_3):
        total = total + other[...].astype(F32)
    k_rows = (total[:, 0:HEAD] * FACTOR).astype(BF16)
    v_rows = total[:, HEAD : 2 * HEAD].astype(BF16)
    k_out[...] = jnp.dot(scatter, k_rows, preferred_element_type=F32).astype(BF16)
    v_out[...] = jnp.dot(scatter, v_rows, preferred_element_type=F32).astype(BF16)
    logits = (part_a[...] + part_b[...]) * closed_ref[...]
    logit_rows = jnp.concatenate([logits, logits], axis=0).astype(BF16)
    for part in range(TOKENS // SLOTS):
        rows = slice(part * SLOTS, (part + 1) * SLOTS)
        logit_out[part : part + 1, :] = nt_dot(logit_rows, scatter[rows])[0:1].astype(BF16)


def whole(count):
    return [pl.BlockSpec(memory_space=pltpu.VMEM)] * count


def params(limit=VMEM_BYTES):
    return pltpu.CompilerParams(vmem_limit_bytes=limit)


def shape(dims, kind=BF16):
    return jax.ShapeDtypeStruct(dims, kind)


def hbm(count):
    return [pl.BlockSpec(memory_space=pltpu.HBM)] * count


def cost(flops):
    return pl.CostEstimate(flops=flops, bytes_accessed=1 << 20, transcendentals=0)


def across(block, step, first):
    def device(y, x, c):
        return (y % 4 * 4 + x % 4) * 2 + c

    pairs = []
    for y in range(4):
        for x in range(4):
            for c in range(2):
                along_x = (c == 0) == first
                target = device(y, x + step, c) if along_x else device(y + step, x, c)
                pairs.append((device(y, x, c), target))
    return lax.ppermute(block, ("y", "x", "c"), pairs)


def local(head_queries, key_projection_rows, value_projection_rows, gate_logit, upstream, picked):
    picked_row = picked.reshape(1, SLOTS)
    swap = [(0, 1), (1, 0)]
    kv_copies = pl.pallas_call(
        pick_kv_kernel,
        out_shape=shape((CHIPS, SLOTS, 2 * HEAD)),
        in_specs=hbm(3),
        out_specs=hbm(1)[0],
        scratch_shapes=[
            pltpu.VMEM((1, SLOTS), jnp.int32),
            pltpu.VMEM((TOKENS, HEAD), BF16),
            pltpu.VMEM((TOKENS, HEAD), BF16),
            pltpu.VMEM((SLOTS, 2 * HEAD), BF16),
            pltpu.SemaphoreType.DMA((3,)),
            pltpu.SemaphoreType.DMA((CHIPS,)),
        ],
        compiler_params=params(VMEM_ALL),
        name="pick_kv",
    )(picked_row, key_projection_rows, value_projection_rows)
    kv_all = lax.all_to_all(kv_copies, ("y", "x"), 0, 0, tiled=True)
    gate_row = gate_logit.reshape(1, TOKENS)
    qs_own = pl.pallas_call(
        pick_q_kernel,
        out_shape=shape((2, CHUNKS, ROWS, HEAD)),
        in_specs=hbm(1) + whole(1) + hbm(2),
        out_specs=whole(1)[0],
        scratch_shapes=[
            pltpu.VMEM((1, SLOTS), jnp.int32),
            pltpu.VMEM((TOKENS, GROUP * HEAD), BF16),
            pltpu.VMEM((TOKENS, GROUP * HEAD), BF16),
            pltpu.SemaphoreType.DMA((3,)),
        ],
        compiler_params=params(),
        cost_estimate=cost(1 << 30),
        name="pick_q",
    )(picked_row, gate_row, head_queries, upstream)
    qs_peer = lax.ppermute(qs_own, "c", swap)
    peer_picked = lax.ppermute(picked_row, "c", swap)
    kc, vc, q_rows, s_rows, stats, raised, pushed, tops, info = pl.pallas_call(
        stats_kernel,
        out_shape=(
            shape((PICKED, HEAD)),
            shape((PICKED, HEAD)),
            shape(((2 * CHUNKS + 1) * ROWS, HEAD)),
            shape(((2 * CHUNKS + 1) * ROWS, HEAD)),
            shape((SPARE + 1, 8, ROWS), F32),
            shape((CHUNKS, KEPT, 2 * ROWS), F32),
            shape((CHUNKS, KEPT, 2 * ROWS), F32),
            shape((CHUNKS, KEPT // PART, 8, 2 * ROWS), F32),
            shape((32,), jnp.int32),
        ),
        in_specs=whole(4),
        out_specs=tuple(whole(8)) + (pl.BlockSpec(memory_space=pltpu.SMEM),),
        scratch_shapes=[pltpu.VMEM((PICKED + SLOTS + KEYS, HEAD), F32)] * 2,
        compiler_params=params(KERNEL_BYTES),
        name="stats",
    )(peer_picked, kv_all, qs_own, qs_peer)
    stats_peer = lax.ppermute(stats, "c", swap)
    comb, deltas = pl.pallas_call(
        combine_kernel,
        out_shape=(shape((SPARE + 1, 8, ROWS), F32), shape((8, SLOTS), F32)),
        in_specs=[pl.BlockSpec(memory_space=pltpu.SMEM)] + whole(2),
        out_specs=tuple(whole(2)),
        compiler_params=params(KERNEL_BYTES),
        name="combine",
    )(info, stats, stats_peer)
    delta_near = lax.ppermute(deltas, "tp", [(i, i ^ 1) for i in range(8)])
    *lines, dq_own, dq_oth = pl.pallas_call(
        grad_kernel,
        out_shape=(shape((4, SLOTS, 2 * HEAD)),) * 4
        + (
            shape((CHUNKS, ROWS, HEAD), F32),
            shape((CHUNKS, ROWS, HEAD)),
        ),
        in_specs=[pl.BlockSpec(memory_space=pltpu.SMEM)] + whole(8),
        out_specs=tuple(whole(6)),
        scratch_shapes=[
            pltpu.VMEM((PICKED + SLOTS, HEAD), F32),
            pltpu.VMEM((PICKED + SLOTS, HEAD), F32),
            pltpu.VMEM((2 * ROWS, HEAD), F32),
        ],
        compiler_params=params(KERNEL_BYTES),
        cost_estimate=cost(1 << 32),
        name="grads",
    )(info, kc, vc, q_rows, s_rows, comb, raised, pushed, tops)
    delta_near, *lines = lax.optimization_barrier((delta_near, *lines))
    deltas = deltas + delta_near
    lines = lines[:1] + [across(lines[k], k, False) for k in (1, 2, 3)]
    sums = [sum(line[j].astype(F32) for line in lines) for j in range(4)]
    delta_far = lax.ppermute(deltas, "tp", [(i, i ^ 4) for i in range(8)])
    dq_peer = lax.ppermute(dq_oth, "c", swap)
    q_out, closed = pl.pallas_call(
        place_q_kernel,
        out_shape=(shape((TOKENS, GROUP * HEAD)), shape((8, SLOTS), F32)),
        in_specs=whole(4),
        out_specs=tuple(whole(2)),
        compiler_params=params(),
        cost_estimate=cost(1 << 29),
        name="place_q",
    )(picked_row, gate_row, dq_own, dq_peer)
    parts = [sums[j].astype(BF16) for j in (1, 2, 3)]
    delta_far, *parts = lax.optimization_barrier((delta_far, *parts))
    arrived = [across(parts[j - 1], j, True) for j in (1, 2, 3)]
    logit_half = deltas + delta_far
    logit_rest = lax.ppermute(logit_half, "tp", [(i, i ^ 2) for i in range(8)])
    k_out, v_out, logit_out = pl.pallas_call(
        place_kv_kernel,
        out_shape=(
            shape((TOKENS, HEAD)),
            shape((TOKENS, HEAD)),
            shape((TOKENS // SLOTS, SLOTS)),
        ),
        in_specs=whole(8),
        out_specs=tuple(whole(3)),
        compiler_params=params(),
        name="place_kv",
    )(picked_row, closed, sums[0], *arrived, logit_half, logit_rest)
    return q_out, k_out, v_out, logit_out.reshape(TOKENS)


def solution(mesh):
    split = Mesh(mesh.devices.reshape(4, 4, 2, 8), ("y", "x", "c", "tp"))
    seq = ("y", "x", "c")
    return jax.shard_map(
        local,
        mesh=split,
        in_specs=(P(seq, "tp"), P(seq, "tp"), P(seq, "tp"), P(seq), P(seq, "tp"), P(seq)),
        out_specs=(P(seq, "tp"), P(seq, "tp"), P(seq, "tp"), P(seq)),
        check_vma=False,
    )
```
